512 devices in a mesh: stream: 16 (over z), pitch: 32 (over y, x, core).
Axes of the slice: x: 4, y: 4, z: 16, core: 2. Of those that a mesh axis runs over, the one named last changes fastest.
Arguments:
- flow_state: float32 [5, 256, 16384], P(None, 'stream', 'pitch'), may hold values from -6 to 6
- residual: float32 [5, 256, 16384], P(None, 'stream', 'pitch'), may hold values from -3 to 3
- spread: float32 [256, 16384], P('stream', 'pitch'), may hold values from 0.02 to 0.2
- diag_inv: float32 [25, 256, 16384], P(None, 'stream', 'pitch'), may hold values from -0.2 to 1, as said below
- lower_jac: float32 [25, 256, 16384], P(None, 'stream', 'pitch'), may hold values from -0.2 to 1.5, as said below
- upper_jac: float32 [25, 256, 16384], P(None, 'stream', 'pitch'), may hold values from -0.2 to 1.5, as said below
- partner: int32 [128], replicated, may hold values from 0 to 127, as said below
Outputs:
- updated: float32 [5, 256, 16384], P(None, 'stream', 'pitch')
The draws below stay inside these ranges and needn't reach their ends.
Inputs may be any that keep to these rules, and one draw needn't show every extreme that they name: `partner`: a permutation of the pitch positions. `diag_inv`: each cell's block has a positive diagonal. `lower_jac`: each cell's block has a positive diagonal. `upper_jac`: each cell's block has a positive diagonal.
All inputs are finite; a program needn't handle non-finite values.
Results may differ from the reference program's by a relative error of at most 0.00012.
Values sent between devices are 32-bit elements; how exact they have to be, the bound alone decides.
A program may use at most 64 MiB of HBM per device.

```python
import math
import jax
import jax.numpy as jnp
from jax import lax

NC = 5
CS = 16
SPANC = 128
STREAMWISE_COUNT = 256
NPITCH = 128
NP = 16384


def shared_diagonal(key):
    return jax.random.uniform(jax.random.fold_in(key, 77), (NC, STREAMWISE_COUNT, NP), jnp.float32, 0.7, 1.0)


def skew_part(key, scale):
    raw_draw = jnp.clip(scale * jax.random.normal(key, (NC, NC, STREAMWISE_COUNT, NP), jnp.float32), -0.1, 0.1)
    return raw_draw - jnp.transpose(raw_draw, (1, 0, 2, 3))


def draw_diag_inv(key, part):
    diagonal_piece = shared_diagonal(key)
    key = jax.random.fold_in(key, 1)
    off_diag = skew_part(key, 0.04)
    identity = jnp.eye(NC, dtype=jnp.float32)[:, :, None, None]
    blocks = identity * diagonal_piece[:, None, :, :] + off_diag
    return blocks.reshape(NC * NC, STREAMWISE_COUNT, NP)


def draw_lower_jac(key, part):
    base_key = key
    key = jax.random.fold_in(key, 2)
    slow_share = 0.5
    return coupling_blocks_keyed(base_key, key, slow_share)


def draw_upper_jac(key, part):
    base_key = key
    key = jax.random.fold_in(key, 3)
    slow_share = 0.5
    return coupling_blocks_keyed(base_key, key, slow_share)


def coupling_blocks_keyed(base_key, private_key, slow_share):
    diagonal_piece = shared_diagonal(base_key)
    selection_key, quick_key, spike_key, offdiagonal_key = jax.random.split(private_key, 4)
    picked = jax.random.uniform(selection_key, (NC, 1, NP), jnp.float32) < slow_share
    slow_gain = 0.3 ** (2.0 / STREAMWISE_COUNT)
    fast_gain = jnp.exp(-1.0 / jax.random.uniform(quick_key, (NC, 1, NP), jnp.float32, 30.0, 50.0))
    retain_fraction = jnp.where(picked, slow_gain, fast_gain)
    spike_events = jax.random.randint(spike_key, (3,), 0, STREAMWISE_COUNT)
    spike_occurs = jnp.sum((jnp.arange(STREAMWISE_COUNT)[:, None] == spike_events[None, :]).astype(jnp.float32), axis=1) > 0.0
    spike_multiplier = jnp.where(spike_occurs, 0.6, 1.0)[None, :, None]
    block_fraction = retain_fraction * spike_multiplier / diagonal_piece
    identity = jnp.eye(NC, dtype=jnp.float32)[:, :, None, None]
    blocks = identity * block_fraction[:, None, :, :] + skew_part(offdiagonal_key, 0.04)
    return blocks.reshape(NC * NC, STREAMWISE_COUNT, NP)


def draw_partner(key, part):
    key = jax.random.fold_in(key, 4)
    return jax.random.permutation(key, NPITCH).astype(jnp.int32)


def steps_of(stream_key, extent, cuts, low, largest):
    def one(position, shards_of):
        draws = jax.random.uniform(jax.random.fold_in(jax.random.fold_in(stream_key, 6), position), (shards_of,), jnp.float32, low / len(cuts), largest / len(cuts))
        return jnp.repeat(jnp.exp(draws), extent[position] // shards_of).reshape((-1,) + (1,) * (len(extent) - position - 1))

    level = one(*cuts[0])
    for cut in cuts[1:]:
        level = level * one(*cut)
    return level


def centred(rng, shape, scale, bound, shards=(), held_as=jnp.bfloat16):
    drawn = scale * jax.random.normal(rng, shape, jnp.float32)
    if shards:
        drawn = drawn * steps_of(rng, shape, shards, -0.22, 0.18)
    return jnp.clip(drawn, -bound, bound).astype(held_as)


def setup_inputs(seed: int = 0) -> dict:
    arg_keys = jax.random.split(jax.random.key(seed), 8)
    flow_state = centred(arg_keys[0], (NC, STREAMWISE_COUNT, NP), 1.0, 6.0, ((1, 16), (2, 32)), jnp.float32)
    residual = centred(arg_keys[1], (NC, STREAMWISE_COUNT, NP), 0.3, 3.0, ((1, 16), (2, 32)), jnp.float32)
    spread = jnp.clip(jnp.exp(math.log(0.2) - 2.3025851 * jax.random.uniform(arg_keys[2], (STREAMWISE_COUNT, NP), jnp.float32) ** steps_of(arg_keys[2], (STREAMWISE_COUNT, NP), ((0, 16), (1, 32)), -0.2, 0.2)), 0.02, 0.2)
    diag_inv = draw_diag_inv(jax.random.fold_in(arg_keys[7], 71), 0)
    lower_jac = draw_lower_jac(jax.random.fold_in(arg_keys[7], 71), 0)
    upper_jac = draw_upper_jac(jax.random.fold_in(arg_keys[7], 71), 0)
    partner = draw_partner(jax.random.fold_in(arg_keys[7], 71), 0)
    return dict(flow_state=flow_state, residual=residual, spread=spread, diag_inv=diag_inv, lower_jac=lower_jac, upper_jac=upper_jac, partner=partner)


def apply_block(matrix, vector):
    return jnp.sum(matrix * vector[None, :, :], axis=1)


def reference(flow_state, residual, spread, diag_inv, lower_jac, upper_jac, partner):
    components, plane_count, cell_count = flow_state.shape
    above = jnp.roll(flow_state, -SPANC, axis=2)
    below = jnp.roll(flow_state, SPANC, axis=2)
    source = residual + spread[None] * (above + below - 2.0 * flow_state)
    interface_plane = STREAMWISE_COUNT // 2 + CS // 2
    rotor_cells = flow_state[:, interface_plane - 1, :].reshape(components, NPITCH, SPANC)
    rotor_ghost = jnp.take(rotor_cells, partner, axis=1).reshape(components, cell_count)
    inverse = diag_inv.reshape(components, components, plane_count, cell_count)
    lower_blocks = lower_jac.reshape(components, components, plane_count, cell_count)
    upper_blocks = upper_jac.reshape(components, components, plane_count, cell_count)
    source = source.at[:, interface_plane, :].add(apply_block(lower_blocks[:, :, interface_plane, :], rotor_ghost))
    plane_ids = jnp.arange(plane_count)
    lower_keep = (plane_ids != interface_plane).astype(jnp.float32)
    upper_keep = (plane_ids != interface_plane - 1).astype(jnp.float32)
    zero_plane = jnp.zeros((components, cell_count), jnp.float32)

    def forward(previous, plane):
        coupled = apply_block(lower_blocks[:, :, plane, :], previous) * lower_keep[plane]
        current = apply_block(inverse[:, :, plane, :], source[:, plane, :] + coupled)
        return current, current

    _, stars = lax.scan(forward, zero_plane, plane_ids)

    def backward(following, plane):
        coupled = apply_block(upper_blocks[:, :, plane, :], following) * upper_keep[plane]
        current = stars[plane] + apply_block(inverse[:, :, plane, :], coupled)
        return current, current

    _, changes = lax.scan(backward, zero_plane, plane_ids, reverse=True)
    return flow_state + jnp.transpose(changes, (1, 0, 2))
```

```python
import jax
import jax.numpy as jnp
from jax import lax
from jax.experimental import pallas as pl
from jax.experimental.pallas import tpu as pltpu
from jax.sharding import PartitionSpec as P

MESH = pl.DeviceIdType.MESH
NC = 5
NS = 16
NPI = 32
CUT = 8
HOPS = 8


def mm(a, b):
    return jnp.stack([sum(a[r, k][None] * b[k] for k in range(NC)) for r in range(NC)])


def mv(a, x):
    return sum(a[:, k] * x[k][None] for k in range(NC))


def kernel(
    flow, res, spr, dinv, low, upp, partner, out,
    flow_v, res_v, spr_v, d_v, l_v, u_v, src_v,
    s_v, t_v, f_v, q_v, p_v, c_v,
    halo_lo, halo_hi, rot, rots, ghost,
    m_d, b_d, w_d, v_d, ww_d, vh, fsend, frecv, bsend, brecv,
    part_s, ld_sem, hs_sem, hr_sem, gs_sem, gr_sem, fs_sem, fr_sem, bs_sem, br_sem,
):
    st = lax.axis_index("stream")
    pt = lax.axis_index("pitch")
    up_s, dn_s = lax.rem(st + 1, NS), lax.rem(st + NS - 1, NS)
    up_p, dn_p = lax.rem(pt + 1, NPI), lax.rem(pt + NPI - 1, NPI)
    is_cut = st == CUT

    loads = [
        pltpu.make_async_copy(h, v, ld_sem.at[i])
        for i, (h, v) in enumerate(
            ((flow, flow_v), (dinv, d_v), (low, l_v), (upp, u_v), (res, res_v), (spr, spr_v))
        )
    ]
    for c in loads:
        c.start()

    barrier = pltpu.get_barrier_semaphore()
    for nb in (up_s, dn_s):
        pl.semaphore_signal(barrier, inc=1, device_id={"stream": nb}, device_id_type=MESH)
    for nb in (up_p, dn_p):
        pl.semaphore_signal(barrier, inc=1, device_id={"pitch": nb}, device_id_type=MESH)

    @pl.when(is_cut)
    def _():
        for d in range(2, NPI - 1):
            pl.semaphore_signal(
                barrier, inc=1, device_id={"pitch": lax.rem(pt + d, NPI)}, device_id_type=MESH
            )

    pl.semaphore_wait(barrier, jnp.where(is_cut, NPI + 1, 4))

    loads[0].wait()

    def halos():
        copies = []
        for h in range(2):
            copies.append(
                pltpu.make_async_remote_copy(
                    flow_v.at[:, pl.ds(h * 32 + 24, 8), :], halo_lo.at[:, h],
                    hs_sem.at[h], hr_sem.at[h], device_id={"pitch": up_p}, device_id_type=MESH,
                )
            )
            copies.append(
                pltpu.make_async_remote_copy(
                    flow_v.at[:, pl.ds(h * 32, 8), :], halo_hi.at[:, h],
                    hs_sem.at[2 + h], hr_sem.at[2 + h], device_id={"pitch": dn_p}, device_id_type=MESH,
                )
            )
        return copies

    for c in halos():
        c.start()

    def rotor_copies():
        return [
            pltpu.make_async_remote_copy(
                rots, rot.at[pt], gs_sem.at[d], gr_sem.at[d],
                device_id={"pitch": lax.rem(pt + d, NPI)}, device_id_type=MESH,
            )
            for d in range(1, NPI)
        ]

    @pl.when(is_cut)
    def _():
        rots[...] = flow_v[:, pl.ds(7, 4, stride=8), :]
        rot[pt] = flow_v[:, pl.ds(7, 4, stride=8), :]
        pltpu.make_async_copy(partner, part_s, ld_sem.at[6]).start()
        for c in rotor_copies():
            c.start()

    for c in loads[1:4]:
        c.wait()

    def block(ref, i):
        return ref[:, pl.ds(i, 8, stride=8), :].reshape(NC, NC, 8, 128)

    def first(i, f):
        s = mm(block(d_v, i), block(l_v, i))
        s_v[i] = s
        f = jnp.where(i == 0, s, mm(s, f))
        f_v[i] = f
        return f

    lax.fori_loop(0, 8, lambda i, _: (first(i, f_v[jnp.maximum(i - 1, 0)]), 0)[1], 0)

    def last(j, _):
        i = 7 - j
        n = jnp.minimum(i + 1, 7)
        t = mm(block(d_v, i), block(u_v, i))
        t_v[i] = t
        q_v[i] = jnp.where(i == 7, t, mm(t, q_v[n]))
        p_v[i] = f_v[i] + jnp.where(i == 7, 0.0, mm(t, p_v[n]))
        return 0

    lax.fori_loop(0, 8, last, 0)

    keep = jnp.where(is_cut, 0.0, 1.0)
    m0, m1 = f_v[7, :, :, 0:4, :], f_v[7, :, :, 4:8, :]
    m_d[...] = mm(m1, m0) * keep
    b0, b1 = q_v[0, :, :, 0:4, :], q_v[0, :, :, 4:8, :]
    b_d[...] = mm(b0, b1) * keep
    w0, w1 = p_v[0, :, :, 0:4, :], p_v[0, :, :, 4:8, :]
    w_d[...] = w0 + mm(b0, mm(w1, m0)) * keep

    for c in loads[4:]:
        c.wait()
    for c in halos():
        c.wait()

    for h in range(2):
        for c in range(4):
            r = h * 32 + c * 8
            mid = flow_v[:, r : r + 8, :]
            lo = halo_lo[:, h] if c == 0 else flow_v[:, r - 8 : r, :]
            hi = halo_hi[:, h] if c == 3 else flow_v[:, r + 8 : r + 16, :]
            src_v[:, r : r + 8, :] = res_v[:, r : r + 8, :] + spr_v[r : r + 8, :][None] * (
                hi + lo - 2.0 * mid
            )

    star = None
    for i in range(8):
        now = mv(block(d_v, i), src_v[:, pl.ds(i, 8, stride=8), :])
        star = now if star is None else now + mv(s_v[i], star)
        c_v[i] = star
    vh[0] = star
    ch = star
    for i in range(6, -1, -1):
        ch = c_v[i] + mv(t_v[i], ch)
        c_v[i] = ch
    vh[1] = ch
    v0, v1 = vh[0, :, 0:4, :], vh[0, :, 4:8, :]
    ww0, ww1 = vh[1, :, 0:4, :], vh[1, :, 4:8, :]
    ghost[...] = v0

    @pl.when(is_cut)
    def _():
        pltpu.make_async_copy(partner, part_s, ld_sem.at[6]).wait()
        for c in rotor_copies():
            c.wait()
        for k in range(4):
            who = part_s[pt * 4 + k]
            ghost[:, k : k + 1, :] = rot[who // 4, :, pl.ds(who % 4, 1), :]

    a1_base = ghost[...]
    v_d[...] = mv(m1, a1_base) + v1
    ww_d[...] = ww0 + mv(b0, mv(w1, v0) + ww1) * keep

    def f_copy(t):
        return pltpu.make_async_remote_copy(
            fsend.at[t], frecv.at[t], fs_sem.at[t], fr_sem.at[t],
            device_id={"stream": up_s}, device_id_type=MESH,
        )

    def b_copy(t):
        return pltpu.make_async_remote_copy(
            bsend.at[t], brecv.at[t], bs_sem.at[t], br_sem.at[t],
            device_id={"stream": dn_s}, device_id_type=MESH,
        )

    a_in = None
    first_keep = jnp.where(lax.rem(st, CUT) == 0, 0.0, 1.0)
    for t in range(HOPS):
        fsend[t] = v_d[...] if t == 0 else mv(m_d[...], a_in) * first_keep + v_d[...]
        f_copy(t).start()
        f_copy(t).wait_recv()
        a_in = frecv[t]
    a_in = a_in * jnp.where(st == 0, 0.0, 1.0)
    y = mv(w_d[...], a_in) + ww_d[...]
    b_in = None
    last_keep = jnp.where(st == NS - 1, 0.0, 1.0)
    for t in range(HOPS):
        bsend[t] = y if t == 0 else mv(b_d[...], b_in) * last_keep + y
        b_copy(t).start()
        b_copy(t).wait_recv()
        b_in = brecv[t]
    b_in = b_in * last_keep

    a1 = mv(m0, a_in) * keep + a1_base
    b_h0 = (mv(b1, b_in) + mv(w1, a1) + ww1) * keep
    vh[0, :, 0:4, :] = a_in
    vh[0, :, 4:8, :] = a1
    vh[1, :, 0:4, :] = b_h0
    vh[1, :, 4:8, :] = b_in
    a_h, b_h = vh[0], vh[1]
    for i in range(8):
        out[:, pl.ds(i, 8, stride=8), :] = (
            flow_v[:, pl.ds(i, 8, stride=8), :] + c_v[i] + mv(p_v[i], a_h) + mv(q_v[i], b_h)
        )
    for t in range(HOPS):
        f_copy(t).wait_send()
        b_copy(t).wait_send()


def to_tiles(x):
    lead = x.shape[:-2]
    x = x.reshape(lead + (2, 8, 4, 128))
    n = len(lead)
    x = jnp.transpose(x, tuple(range(n)) + (n, n + 2, n + 1, n + 3))
    return x.reshape(lead + (64, 128))


def from_tiles(x):
    lead = x.shape[:-2]
    x = x.reshape(lead + (2, 4, 8, 128))
    n = len(lead)
    x = jnp.transpose(x, tuple(range(n)) + (n, n + 2, n + 1, n + 3))
    return x.reshape(lead + (16, 512))


def local(flow_state, residual, spread, diag_inv, lower_jac, upper_jac, partner):
    f32 = jnp.float32
    vm = lambda *s: pltpu.VMEM(s, f32)
    dma = lambda n: pltpu.SemaphoreType.DMA((n,))
    hbm = pl.BlockSpec(memory_space=pltpu.HBM)
    updated = pl.pallas_call(
        kernel,
        out_shape=jax.ShapeDtypeStruct((NC, 64, 128), f32),
        in_specs=[hbm] * 7,
        out_specs=pl.BlockSpec(memory_space=pltpu.VMEM),
        scratch_shapes=[
            vm(5, 64, 128), vm(5, 64, 128), vm(64, 128), vm(25, 64, 128), vm(25, 64, 128), vm(25, 64, 128), vm(5, 64, 128),
            vm(8, 5, 5, 8, 128), vm(8, 5, 5, 8, 128), vm(8, 5, 5, 8, 128), vm(8, 5, 5, 8, 128), vm(8, 5, 5, 8, 128), vm(8, 5, 8, 128),
            vm(5, 2, 8, 128), vm(5, 2, 8, 128), vm(NPI, 5, 4, 128), vm(5, 4, 128), vm(5, 4, 128),
            vm(5, 5, 4, 128), vm(5, 5, 4, 128), vm(5, 5, 4, 128), vm(5, 4, 128), vm(5, 4, 128), vm(2, 5, 8, 128),
            vm(HOPS, 5, 4, 128), vm(HOPS, 5, 4, 128), vm(HOPS, 5, 4, 128), vm(HOPS, 5, 4, 128),
            pltpu.SMEM((128,), jnp.int32), dma(7), dma(4), dma(4), dma(NPI), dma(NPI), dma(HOPS), dma(HOPS), dma(HOPS), dma(HOPS),
        ],
        compiler_params=pltpu.CompilerParams(
            collective_id=0, has_side_effects=True, vmem_limit_bytes=60 * 1024 * 1024
        ),
        name="lusgs",
    )(
        to_tiles(flow_state), to_tiles(residual), to_tiles(spread), to_tiles(diag_inv),
        to_tiles(lower_jac), to_tiles(upper_jac), partner,
    )
    return from_tiles(updated)


def solution(mesh):
    blocks = P(None, "stream", "pitch")
    in_specs = (blocks, blocks, P("stream", "pitch"), blocks, blocks, blocks, P())
    return jax.shard_map(local, mesh=mesh, in_specs=in_specs, out_specs=blocks, check_vma=False)
```

```python
import jax
import jax.numpy as jnp
from jax import lax
from jax.experimental import pallas as pl
from jax.experimental.pallas import tpu as pltpu
from jax.sharding import PartitionSpec as P

MESH = pl.DeviceIdType.MESH
NC = 5
NS = 16
NPI = 32
CUT = 8
MID = 5


def mm(a, b):
    return jnp.stack([sum(a[r, k][None] * b[k] for k in range(NC)) for r in range(NC)])


def mv(a, x):
    return sum(a[:, k] * x[k][None] for k in range(NC))


def kernel(
    flow, res, spr, dinv, low, upp, partner, out,
    flow_v, res_v, spr_v, d_v, l_v, u_v, src_v,
    s_v, t_v, f_v, q_v, p_v, c_v,
    halo_lo, halo_hi, rot, rots, ghost,
    maps, vecs, vh, c_maps, c_vecs, answer, in_a, in_b, side_b, side_y, y_out,
    part_s, ld_sem, hs_sem, hr_sem, gs_sem, gr_sem,
    ms_sem, cm_sem, vs_sem, cv_sem, sbs_sem, sbr_sem, sys_sem, syr_sem, as_sem, ar_sem, bs_sem, br_sem,
):
    st = lax.axis_index("stream")
    pt = lax.axis_index("pitch")
    up_p, dn_p = lax.rem(pt + 1, NPI), lax.rem(pt + NPI - 1, NPI)
    is_cut = st == CUT
    pos = lax.rem(st, CUT)
    base = st - pos
    core = lax.rem(pt, 2)
    pair = pt - core
    centre = base + MID
    before = lax.rem(st + NS - CUT + MID, NS)
    is_mid = (pos == MID) & (core == 1)
    left = pos < MID

    def to(stream, pitch):
        return dict(device_id=(stream, pitch), device_id_type=MESH)

    loads = [
        pltpu.make_async_copy(h, v, ld_sem.at[i])
        for i, (h, v) in enumerate(
            ((flow, flow_v), (dinv, d_v), (low, l_v), (upp, u_v), (res, res_v), (spr, spr_v))
        )
    ]

    barrier = pltpu.get_barrier_semaphore()
    for nb in (up_p, dn_p):
        pl.semaphore_signal(barrier, inc=1, **to(st, nb))

    @pl.when(jnp.logical_not(is_mid))
    def _():
        pl.semaphore_signal(barrier, inc=1, **to(centre, pair + 1))

    @pl.when(pos == 0)
    def _():
        pl.semaphore_signal(barrier, inc=1, **to(before, pair + 1))

    @pl.when(left)
    def _():
        for q in range(MID):
            @pl.when(pos != q)
            def _():
                pl.semaphore_signal(barrier, inc=1, **to(base + q, pt))

    @pl.when(is_mid)
    def _():
        for q in range(CUT + 1):
            for k in range(2):
                if (q, k) != (MID, 1):
                    pl.semaphore_signal(barrier, inc=1, **to(lax.rem(base + q, NS), pair + k))

    @pl.when(is_cut)
    def _():
        for d in range(2, NPI - 1):
            pl.semaphore_signal(barrier, inc=1, **to(st, lax.rem(pt + d, NPI)))

    for c in loads:
        c.start()

    expected = (
        jnp.where(is_cut, NPI - 1, 2) + jnp.where(is_mid, 2 * CUT + 1, 1)
        + jnp.where(pos == 0, 1, 0) + jnp.where(left, MID - 1, 0)
    )
    pl.semaphore_wait(barrier, expected)

    loads[0].wait()

    def halos():
        copies = []
        for h in range(2):
            copies.append(
                pltpu.make_async_remote_copy(
                    flow_v.at[:, pl.ds(h * 32 + 24, 8), :], halo_lo.at[:, h],
                    hs_sem.at[h], hr_sem.at[h], **to(st, up_p),
                )
            )
            copies.append(
                pltpu.make_async_remote_copy(
                    flow_v.at[:, pl.ds(h * 32, 8), :], halo_hi.at[:, h],
                    hs_sem.at[2 + h], hr_sem.at[2 + h], **to(st, dn_p),
                )
            )
        return copies

    for c in halos():
        c.start()

    def rotor_copies():
        return [
            pltpu.make_async_remote_copy(
                rots, rot.at[pt], gs_sem.at[d], gr_sem.at[d], **to(st, lax.rem(pt + d, NPI))
            )
            for d in range(1, NPI)
        ]

    @pl.when(is_cut)
    def _():
        rots[...] = flow_v[:, pl.ds(7, 4, stride=8), :]
        rot[pt] = flow_v[:, pl.ds(7, 4, stride=8), :]
        pltpu.make_async_copy(partner, part_s, ld_sem.at[6]).start()
        for c in rotor_copies():
            c.start()

    for c in loads[1:4]:
        c.wait()

    def block(ref, i):
        return ref[:, pl.ds(i, 8, stride=8), :].reshape(NC, NC, 8, 128)

    def first(i, f):
        s = mm(block(d_v, i), block(l_v, i))
        s_v[i] = s
        f = jnp.where(i == 0, s, mm(s, f))
        f_v[i] = f
        return f

    lax.fori_loop(0, 8, lambda i, _: (first(i, f_v[jnp.maximum(i - 1, 0)]), 0)[1], 0)

    keep = jnp.where(is_cut, 0.0, 1.0)
    m0, m1 = f_v[7, :, :, 0:4, :], f_v[7, :, :, 4:8, :]
    maps[0] = mm(m1, m0)

    def map_copy(k, stream=centre):
        slot = pos
        return pltpu.make_async_remote_copy(
            maps.at[k], c_maps.at[core, slot, k], ms_sem.at[k], cm_sem.at[core, slot, k], **to(stream, pair + 1)
        )

    near = (pos >= MID) & jnp.logical_not(is_mid)

    @pl.when(((pos > 0) & left) | near)
    def _():
        map_copy(0).start()

    def last(j, _):
        i = 7 - j
        n = jnp.minimum(i + 1, 7)
        t = mm(block(d_v, i), block(u_v, i))
        t_v[i] = t
        q_v[i] = jnp.where(i == 7, t, mm(t, q_v[n]))
        p_v[i] = f_v[i] + jnp.where(i == 7, 0.0, mm(t, p_v[n]))
        return 0

    lax.fori_loop(0, 8, last, 0)

    b0, b1 = q_v[0, :, :, 0:4, :], q_v[0, :, :, 4:8, :]
    maps[1] = mm(b0, b1)
    w0, w1 = p_v[0, :, :, 0:4, :], p_v[0, :, :, 4:8, :]
    maps[2] = (w0 + mm(b0, mm(w1, m0)) * keep) * jnp.where(st == 0, 0.0, 1.0)

    def side_b_copy(q):
        return pltpu.make_async_remote_copy(
            maps.at[1], side_b.at[pos], sbs_sem.at[q], sbr_sem.at[pos], **to(base + q, pt)
        )

    @pl.when(near)
    def _():
        map_copy(1).start()
        map_copy(2).start()

    @pl.when(pos == 0)
    def _():
        map_copy(2, before).start()

    for q in range(MID - 1):
        @pl.when(left & (pos > q))
        def _():
            side_b_copy(q).start()

    for c in loads[4:]:
        c.wait()
    for c in halos():
        c.wait()

    for h in range(2):
        for c in range(4):
            r = h * 32 + c * 8
            mid = flow_v[:, r : r + 8, :]
            lo = halo_lo[:, h] if c == 0 else flow_v[:, r - 8 : r, :]
            hi = halo_hi[:, h] if c == 3 else flow_v[:, r + 8 : r + 16, :]
            src_v[:, r : r + 8, :] = res_v[:, r : r + 8, :] + spr_v[r : r + 8, :][None] * (
                hi + lo - 2.0 * mid
            )

    star = None
    for i in range(8):
        now = mv(block(d_v, i), src_v[:, pl.ds(i, 8, stride=8), :])
        star = now if star is None else now + mv(s_v[i], star)
        c_v[i] = star
    vh[0] = star
    v0, v1 = vh[0, :, 0:4, :], vh[0, :, 4:8, :]
    ghost[...] = v0

    def v_copy():
        return pltpu.make_async_remote_copy(
            vecs.at[0], c_vecs.at[core, pos, 0], vs_sem.at[0], cv_sem.at[core, pos, 0], **to(centre, pair + 1)
        )

    def w_copy(stream, slot):
        return pltpu.make_async_remote_copy(
            vecs.at[1], c_vecs.at[core, slot, 1], vs_sem.at[1], cv_sem.at[core, slot, 1], **to(stream, pair + 1)
        )

    @pl.when(jnp.logical_not(is_cut))
    def _():
        vecs[0] = mv(m1, v0) + v1

        @pl.when(jnp.logical_not(is_mid))
        def _():
            v_copy().start()

    ch = star
    for i in range(6, -1, -1):
        ch = c_v[i] + mv(t_v[i], ch)
        c_v[i] = ch
    vh[1] = ch
    ww0, ww1 = vh[1, :, 0:4, :], vh[1, :, 4:8, :]
    vecs[1] = (ww0 + mv(b0, mv(w1, v0) + ww1) * keep) * jnp.where(st == 0, 0.0, 1.0)

    @pl.when(near)
    def _():
        w_copy(centre, pos).start()

    @pl.when(pos == 0)
    def _():
        w_copy(before, 0).start()

    @pl.when(is_cut)
    def _():
        pltpu.make_async_copy(partner, part_s, ld_sem.at[6]).wait()
        for c in rotor_copies():
            c.wait()
        for k in range(4):
            who = part_s[pt * 4 + k]
            ghost[:, k : k + 1, :] = rot[who // 4, :, pl.ds(who % 4, 1), :]
        vecs[0] = mv(m1, ghost[...]) + v1
        v_copy().start()

    def a_copy(k, q):
        return pltpu.make_async_remote_copy(
            answer.at[0, k, q], in_a, as_sem.at[k, q], ar_sem.at[0], **to(lax.rem(base + q, NS), pair + k)
        )

    def b_copy(k, q):
        return pltpu.make_async_remote_copy(
            answer.at[1, k, max(q, MID - 1)], in_b, bs_sem.at[k, q], br_sem.at[0], **to(base + q, pair + k)
        )

    def arrived_map(k, q, m):
        pltpu.make_async_copy(maps.at[m], c_maps.at[k, q, m], cm_sem.at[k, q, m]).wait()

    def arrived_vec(k, q, m):
        pltpu.make_async_copy(vecs.at[m], c_vecs.at[k, q, m], cv_sem.at[k, q, m]).wait()

    a_sent = [(k, q) for q in range(1, CUT + 1) for k in range(2) if (k, q) != (1, MID)]
    b_sent = [(k, q) for q in range(CUT) for k in range(2) if (k, q) != (1, MID)]

    @pl.when(is_mid)
    def _():
        c_maps[1, MID] = maps[...]
        c_vecs[1, MID] = vecs[...]
        for k in range(2):
            for q in range(MID):
                if q:
                    arrived_map(k, q, 0)
                arrived_vec(k, q, 0)
        a = [c_vecs[0, 0, 0], c_vecs[1, 0, 0]]
        for q in range(1, MID + 1):
            for k in range(2):
                answer[0, k, q] = a[k]
                if q < MID:
                    a_copy(k, q).start()
                    a[k] = mv(c_maps[k, q, 0], a[k]) + c_vecs[k, q, 0]
        for k in range(2):
            for q in range(MID, CUT):
                if (k, q) != (1, MID):
                    for m in range(3):
                        arrived_map(k, q, m)
                    for m in range(2):
                        arrived_vec(k, q, m)
            arrived_map(k, 0, 2)
            arrived_vec(k, 0, 1)
        for q in range(MID, CUT):
            for k in range(2):
                a[k] = mv(c_maps[k, q, 0], a[k]) + c_vecs[k, q, 0]
                answer[0, k, q + 1] = a[k]
        b = [None, None]
        for k in range(2):
            b[k] = mv(c_maps[k, 0, 2], a[k]) + c_vecs[k, 0, 1]
            answer[1, k, CUT - 1] = b[k]
        for q in range(CUT - 1, MID - 1, -1):
            for k in range(2):
                b[k] = mv(c_maps[k, q, 1], b[k]) + mv(c_maps[k, q, 2], answer[0, k, q]) + c_vecs[k, q, 1]
                answer[1, k, q - 1] = b[k]
        for k, q in b_sent:
            b_copy(k, q).start()
        for k, q in a_sent:
            if q >= MID:
                a_copy(k, q).start()
        in_a[...] = answer[0, 1, MID]
        in_b[...] = answer[1, 1, MID]

    @pl.when(jnp.logical_not(is_mid))
    def _():
        a_copy(0, 1).wait_recv()

    a_in = in_a[...] * jnp.where(st == 0, 0.0, 1.0)

    def side_y_copy(q):
        return pltpu.make_async_remote_copy(
            y_out, side_y.at[pos], sys_sem.at[q], syr_sem.at[pos], **to(base + q, pt)
        )

    @pl.when(left & (pos > 0))
    def _():
        y_out[...] = mv(maps[2], a_in) + vecs[1]
        for q in range(MID - 1):
            @pl.when(pos > q)
            def _():
                side_y_copy(q).start()

    for e in range(1, MID):
        @pl.when(pos < e)
        def _():
            pltpu.make_async_copy(maps.at[1], side_b.at[e], sbr_sem.at[e]).wait()
            pltpu.make_async_copy(y_out, side_y.at[e], syr_sem.at[e]).wait()

    @pl.when(jnp.logical_not(is_mid))
    def _():
        b_copy(0, 0).wait_recv()

    for e in range(MID - 1, 0, -1):
        @pl.when(pos < e)
        def _():
            in_b[...] = mv(side_b[e], in_b[...]) + side_y[e]

    b_in = in_b[...] * jnp.where(st == NS - 1, 0.0, 1.0)

    a1 = jnp.where(is_cut, ghost[...], mv(m0, a_in) + v0)
    b_h0 = (mv(b1, b_in) + mv(w1, a1) + ww1) * keep
    vh[0, :, 0:4, :] = a_in
    vh[0, :, 4:8, :] = a1
    vh[1, :, 0:4, :] = b_h0
    vh[1, :, 4:8, :] = b_in
    a_h, b_h = vh[0], vh[1]
    for i in range(8):
        out[:, pl.ds(i, 8, stride=8), :] = (
            flow_v[:, pl.ds(i, 8, stride=8), :] + c_v[i] + mv(p_v[i], a_h) + mv(q_v[i], b_h)
        )

    @pl.when(((pos > 0) & left) | near)
    def _():
        map_copy(0).wait_send()

    @pl.when(near)
    def _():
        map_copy(1).wait_send()

    @pl.when(near | (pos == 0))
    def _():
        map_copy(2).wait_send()
        w_copy(centre, pos).wait_send()

    @pl.when(jnp.logical_not(is_mid))
    def _():
        v_copy().wait_send()

    for q in range(MID - 1):
        @pl.when(left & (pos > q))
        def _():
            side_b_copy(q).wait_send()
            side_y_copy(q).wait_send()

    @pl.when(is_mid)
    def _():
        for k, q in a_sent:
            a_copy(k, q).wait_send()
        for k, q in b_sent:
            b_copy(k, q).wait_send()


def to_tiles(x):
    lead = x.shape[:-2]
    x = x.reshape(lead + (2, 8, 4, 128))
    n = len(lead)
    x = jnp.transpose(x, tuple(range(n)) + (n, n + 2, n + 1, n + 3))
    return x.reshape(lead + (64, 128))


def from_tiles(x):
    lead = x.shape[:-2]
    x = x.reshape(lead + (2, 4, 8, 128))
    n = len(lead)
    x = jnp.transpose(x, tuple(range(n)) + (n, n + 2, n + 1, n + 3))
    return x.reshape(lead + (16, 512))


def local(flow_state, residual, spread, diag_inv, lower_jac, upper_jac, partner):
    f32 = jnp.float32
    vm = lambda *s: pltpu.VMEM(s, f32)
    dma = lambda *n: pltpu.SemaphoreType.DMA(n)
    hbm = pl.BlockSpec(memory_space=pltpu.HBM)
    updated = pl.pallas_call(
        kernel,
        out_shape=jax.ShapeDtypeStruct((NC, 64, 128), f32),
        in_specs=[hbm] * 7,
        out_specs=pl.BlockSpec(memory_space=pltpu.VMEM),
        scratch_shapes=[
            vm(5, 64, 128), vm(5, 64, 128), vm(64, 128), vm(25, 64, 128), vm(25, 64, 128), vm(25, 64, 128), vm(5, 64, 128),
            vm(8, 5, 5, 8, 128), vm(8, 5, 5, 8, 128), vm(8, 5, 5, 8, 128), vm(8, 5, 5, 8, 128), vm(8, 5, 5, 8, 128), vm(8, 5, 8, 128),
            vm(5, 2, 8, 128), vm(5, 2, 8, 128), vm(NPI, 5, 4, 128), vm(5, 4, 128), vm(5, 4, 128),
            vm(3, 5, 5, 4, 128), vm(2, 5, 4, 128), vm(2, 5, 8, 128),
            vm(2, CUT, 3, 5, 5, 4, 128), vm(2, CUT, 2, 5, 4, 128), vm(2, 2, CUT + 1, 5, 4, 128),
            vm(5, 4, 128), vm(5, 4, 128), vm(MID, 5, 5, 4, 128), vm(MID, 5, 4, 128), vm(5, 4, 128),
            pltpu.SMEM((128,), jnp.int32), dma(7), dma(4), dma(4), dma(NPI), dma(NPI),
            dma(3), dma(2, CUT, 3), dma(2), dma(2, CUT, 2), dma(MID), dma(MID), dma(MID), dma(MID),
            dma(2, CUT + 1), dma(1), dma(2, CUT + 1), dma(1),
        ],
        compiler_params=pltpu.CompilerParams(
            collective_id=0, has_side_effects=True, vmem_limit_bytes=60 * 1024 * 1024
        ),
        name="lusgs",
    )(
        to_tiles(flow_state), to_tiles(residual), to_tiles(spread), to_tiles(diag_inv),
        to_tiles(lower_jac), to_tiles(upper_jac), partner,
    )
    return from_tiles(updated)


def solution(mesh):
    blocks = P(None, "stream", "pitch")
    in_specs = (blocks, blocks, P("stream", "pitch"), blocks, blocks, blocks, P())
    return jax.shard_map(local, mesh=mesh, in_specs=in_specs, out_specs=blocks, check_vma=False)
```

```python
import jax
import jax.numpy as jnp
from jax import lax
from jax.experimental import pallas as pl
from jax.experimental.pallas import tpu as pltpu
from jax.sharding import PartitionSpec as P

MESH = pl.DeviceIdType.MESH
NC = 5
NS = 16
NPI = 32
CUT = 8
ROW = 8
MID = 5


def mm(a, b):
    return jnp.stack([sum(a[r, k][None] * b[k] for k in range(NC)) for r in range(NC)])


def mv(a, x):
    return sum(a[:, k] * x[k][None] for k in range(NC))


def kernel(
    flow, res, spr, dinv, low, upp, partner, out,
    flow_v, res_v, spr_v, d_v, l_v, u_v, src_v,
    s_v, t_v, f_v, q_v, p_v, c_v,
    halo_lo, halo_hi, rot, rots, chosen, facing, ghost,
    maps, vecs, vh, c_maps, c_vecs, answer, in_a, in_b, side_b, side_y, y_out,
    part_s, ld_sem, hs_sem, hr_sem, gs_sem, gr_sem, xs_sem, xr_sem, ready,
    ms_sem, cm_sem, vs_sem, cv_sem, sbs_sem, sbr_sem, sys_sem, syr_sem, as_sem, ar_sem, bs_sem, br_sem,
):
    st = lax.axis_index("stream")
    pt = lax.axis_index("pitch")
    up_p, dn_p = lax.rem(pt + 1, NPI), lax.rem(pt + NPI - 1, NPI)
    is_cut = st == CUT
    pos = lax.rem(st, CUT)
    base = st - pos
    core = lax.rem(pt, 2)
    pair = pt - core
    centre = base + MID
    before = lax.rem(st + NS - CUT + MID, NS)
    is_mid = (pos == MID) & (core == 1)
    left = pos < MID
    near = (pos >= MID) & jnp.logical_not(is_mid)
    row = pt // ROW
    row_peers = [row * ROW + lax.rem(pt + d, ROW) for d in range(1, ROW)]
    column_peers = [lax.rem(pt + d * ROW, NPI) for d in range(1, NPI // ROW)]

    def to(stream, pitch):
        return dict(device_id=(stream, pitch), device_id_type=MESH)

    loads = [
        pltpu.make_async_copy(h, v, ld_sem.at[i])
        for i, (h, v) in enumerate(
            ((flow, flow_v), (dinv, d_v), (low, l_v), (upp, u_v), (res, res_v), (spr, spr_v))
        )
    ]

    loads[0].start()
    barrier = pltpu.get_barrier_semaphore()
    for nb in (up_p, dn_p):
        pl.semaphore_signal(barrier, inc=1, **to(st, nb))

    @pl.when(left)
    def _():
        pl.semaphore_signal(barrier, inc=1, **to(centre, pair + 1))
        for q in range(1, MID):
            @pl.when(pos < q)
            def _():
                pl.semaphore_signal(barrier, inc=1, **to(base + q, pt))

    @pl.when(is_mid)
    def _():
        for q in range(MID, CUT):
            for k in range(2):
                if (q, k) != (MID, 1):
                    pl.semaphore_signal(barrier, inc=1, **to(base + q, pair + k))

        @pl.when(base == 0)
        def _():
            for k in range(2):
                pl.semaphore_signal(barrier, inc=1, **to(CUT, pair + k))

    @pl.when(is_cut)
    def _():
        for nb in row_peers + column_peers:
            pl.semaphore_signal(barrier, inc=1, **to(st, nb))

    for c in loads[1:]:
        c.start()

    expected = (
        2 + jnp.where(is_cut, len(row_peers) + len(column_peers) + 1, 0) + jnp.where(is_mid, 2 * MID, 0)
        + jnp.where(near, 1, 0) + jnp.where(left, pos, 0)
    )
    pl.semaphore_wait(barrier, expected)

    @pl.when(is_mid)
    def _():
        for q in range(MID):
            for k in range(2):
                pl.semaphore_signal(ready, inc=1, **to(base + q, pair + k))

    loads[0].wait()

    def halos():
        copies = []
        for h in range(2):
            copies.append(
                pltpu.make_async_remote_copy(
                    flow_v.at[:, pl.ds(h * 32 + 24, 8), :], halo_lo.at[:, h],
                    hs_sem.at[h], hr_sem.at[h], **to(st, up_p),
                )
            )
            copies.append(
                pltpu.make_async_remote_copy(
                    flow_v.at[:, pl.ds(h * 32, 8), :], halo_hi.at[:, h],
                    hs_sem.at[2 + h], hr_sem.at[2 + h], **to(st, dn_p),
                )
            )
        return copies

    for c in halos():
        c.start()

    def row_copies():
        return [
            pltpu.make_async_remote_copy(
                rots, rot.at[lax.rem(pt, ROW)], gs_sem.at[d], gr_sem.at[d], **to(st, nb)
            )
            for d, nb in enumerate(row_peers)
        ]

    def column_copies():
        return [
            pltpu.make_async_remote_copy(
                chosen.at[d], facing.at[row], xs_sem.at[d], xr_sem.at[d], **to(st, nb)
            )
            for d, nb in enumerate(column_peers)
        ]

    def choose(target, nb):
        for k in range(4):
            who = part_s[nb * 4 + k]
            target[:, k : k + 1, :] = rot[lax.rem(who // 4, ROW), :, pl.ds(lax.rem(who, 4), 1), :]

    @pl.when(is_cut)
    def _():
        rots[...] = flow_v[:, pl.ds(7, 4, stride=8), :]
        rot[lax.rem(pt, ROW)] = flow_v[:, pl.ds(7, 4, stride=8), :]
        pltpu.make_async_copy(partner, part_s, ld_sem.at[6]).start()
        for c in row_copies():
            c.start()

    for c in loads[1:4]:
        c.wait()

    def block(ref, i):
        return ref[:, pl.ds(i, 8, stride=8), :].reshape(NC, NC, 8, 128)

    def first(i, f):
        s = mm(block(d_v, i), block(l_v, i))
        s_v[i] = s
        f = jnp.where(i == 0, s, mm(s, f))
        f_v[i] = f
        return f

    lax.fori_loop(0, 8, lambda i, _: (first(i, f_v[jnp.maximum(i - 1, 0)]), 0)[1], 0)

    keep = jnp.where(is_cut, 0.0, 1.0)
    m0, m1 = f_v[7, :, :, 0:4, :], f_v[7, :, :, 4:8, :]
    maps[0] = mm(m1, m0)

    def map_copy(k, stream=centre):
        slot = pos
        return pltpu.make_async_remote_copy(
            maps.at[k], c_maps.at[core, slot, k], ms_sem.at[k], cm_sem.at[core, slot, k], **to(stream, pair + 1)
        )

    @pl.when(near)
    def _():
        map_copy(0).start()

    def last(j, _):
        i = 7 - j
        n = jnp.minimum(i + 1, 7)
        t = mm(block(d_v, i), block(u_v, i))
        t_v[i] = t
        q_v[i] = jnp.where(i == 7, t, mm(t, q_v[n]))
        p_v[i] = f_v[i] + jnp.where(i == 7, 0.0, mm(t, p_v[n]))
        return 0

    lax.fori_loop(0, 8, last, 0)

    b0, b1 = q_v[0, :, :, 0:4, :], q_v[0, :, :, 4:8, :]
    maps[1] = mm(b0, b1)
    w0, w1 = p_v[0, :, :, 0:4, :], p_v[0, :, :, 4:8, :]
    maps[2] = w0 + mm(b0, mm(w1, m0)) * keep

    def side_b_copy(q):
        return pltpu.make_async_remote_copy(
            maps.at[1], side_b.at[pos], sbs_sem.at[q], sbr_sem.at[pos], **to(base + q, pt)
        )

    @pl.when(near)
    def _():
        map_copy(1).start()
        map_copy(2).start()

    @pl.when(is_cut)
    def _():
        map_copy(2, before).start()

    for q in range(MID - 1):
        @pl.when(left & (pos > q))
        def _():
            side_b_copy(q).start()

    for c in loads[4:]:
        c.wait()
    for c in halos():
        c.wait()

    for h in range(2):
        for c in range(4):
            r = h * 32 + c * 8
            mid = flow_v[:, r : r + 8, :]
            lo = halo_lo[:, h] if c == 0 else flow_v[:, r - 8 : r, :]
            hi = halo_hi[:, h] if c == 3 else flow_v[:, r + 8 : r + 16, :]
            src_v[:, r : r + 8, :] = res_v[:, r : r + 8, :] + spr_v[r : r + 8, :][None] * (
                hi + lo - 2.0 * mid
            )

    star = None
    for i in range(8):
        now = mv(block(d_v, i), src_v[:, pl.ds(i, 8, stride=8), :])
        star = now if star is None else now + mv(s_v[i], star)
        c_v[i] = star
    vh[0] = star
    v0, v1 = vh[0, :, 0:4, :], vh[0, :, 4:8, :]
    ghost[...] = v0

    def v_copy():
        return pltpu.make_async_remote_copy(
            vecs.at[0], c_vecs.at[core, pos, 0], vs_sem.at[0], cv_sem.at[core, pos, 0], **to(centre, pair + 1)
        )

    def w_copy(stream, slot):
        return pltpu.make_async_remote_copy(
            vecs.at[1], c_vecs.at[core, slot, 1], vs_sem.at[1], cv_sem.at[core, slot, 1], **to(stream, pair + 1)
        )

    @pl.when(jnp.logical_not(is_cut))
    def _():
        vecs[0] = mv(m1, v0) + v1

        @pl.when(near)
        def _():
            v_copy().start()

    ch = star
    for i in range(6, -1, -1):
        ch = c_v[i] + mv(t_v[i], ch)
        c_v[i] = ch
    vh[1] = ch
    ww0, ww1 = vh[1, :, 0:4, :], vh[1, :, 4:8, :]
    vecs[1] = ww0 + mv(b0, mv(w1, v0) + ww1) * keep

    @pl.when(near)
    def _():
        w_copy(centre, pos).start()

    @pl.when(is_cut)
    def _():
        w_copy(before, 0).start()

    @pl.when(left & jnp.logical_not(is_cut))
    def _():
        pl.semaphore_wait(ready, 1)
        v_copy().start()

        @pl.when(pos > 0)
        def _():
            map_copy(0).start()

    @pl.when(is_cut)
    def _():
        pltpu.make_async_copy(partner, part_s, ld_sem.at[6]).wait()
        for c in row_copies():
            c.wait()
        choose(facing.at[row], pt)
        for d, c in enumerate(column_copies()):
            choose(chosen.at[d], column_peers[d])
            c.start()

    @pl.when(is_cut)
    def _():
        for c in column_copies():
            c.wait()
        for k in range(4):
            who = part_s[pt * 4 + k]
            ghost[:, k : k + 1, :] = facing[who // (4 * ROW), :, pl.ds(k, 1), :]
        vecs[0] = mv(m1, ghost[...]) + v1
        pl.semaphore_wait(ready, 1)
        v_copy().start()

    def a_copy(k, q):
        return pltpu.make_async_remote_copy(
            answer.at[0, k, q], in_a, as_sem.at[k, q], ar_sem.at[0], **to(lax.rem(base + q, NS), pair + k)
        )

    def b_copy(k, q):
        return pltpu.make_async_remote_copy(
            answer.at[1, k, max(q, MID - 1)], in_b, bs_sem.at[k, q], br_sem.at[0], **to(base + q, pair + k)
        )

    def arrived_map(k, q, m):
        pltpu.make_async_copy(maps.at[m], c_maps.at[k, q, m], cm_sem.at[k, q, m]).wait()

    def arrived_vec(k, q, m):
        pltpu.make_async_copy(vecs.at[m], c_vecs.at[k, q, m], cv_sem.at[k, q, m]).wait()

    a_sent = [(k, q) for q in range(1, CUT + 1) for k in range(2) if (k, q) != (1, MID)]
    b_sent = [(k, q) for q in range(CUT) for k in range(2) if (k, q) != (1, MID)]

    @pl.when(is_mid)
    def _():
        c_maps[1, MID] = maps[...]
        c_vecs[1, MID] = vecs[...]
        for k in range(2):
            for q in range(MID):
                if q:
                    arrived_map(k, q, 0)
                arrived_vec(k, q, 0)
        a = [c_vecs[0, 0, 0], c_vecs[1, 0, 0]]
        for q in range(1, MID + 1):
            for k in range(2):
                answer[0, k, q] = a[k]
                if q < MID:
                    a_copy(k, q).start()
                    a[k] = mv(c_maps[k, q, 0], a[k]) + c_vecs[k, q, 0]
        for k in range(2):
            for q in range(MID, CUT):
                if (k, q) != (1, MID):
                    for m in range(3):
                        arrived_map(k, q, m)
                    for m in range(2):
                        arrived_vec(k, q, m)

        @pl.when(base == 0)
        def _():
            for k in range(2):
                arrived_map(k, 0, 2)

        @pl.when(base != 0)
        def _():
            for k in range(2):
                c_maps[k, 0, 2] = jnp.zeros((NC, NC, 4, 128), jnp.float32)
                c_vecs[k, 0, 1] = jnp.zeros((NC, 4, 128), jnp.float32)

        for q in range(MID, CUT):
            for k in range(2):
                a[k] = mv(c_maps[k, q, 0], a[k]) + c_vecs[k, q, 0]
                answer[0, k, q + 1] = a[k]
        b, g = [None, None], [None, None]
        for k in range(2):
            b[k] = mv(c_maps[k, 0, 2], a[k])
            answer[1, k, CUT - 1] = b[k]
        for q in range(CUT - 1, MID - 1, -1):
            for k in range(2):
                b[k] = mv(c_maps[k, q, 1], b[k]) + mv(c_maps[k, q, 2], answer[0, k, q]) + c_vecs[k, q, 1]
                answer[1, k, q - 1] = b[k]
                c_maps[k, q - MID, 1] = c_maps[k, q, 1] if q == CUT - 1 else mm(c_maps[k, q, 1], c_maps[k, q + 1 - MID, 1])

        @pl.when(base == 0)
        def _():
            for k in range(2):
                arrived_vec(k, 0, 1)

        for q in range(MID - 1, CUT):
            for k in range(2):
                w = c_vecs[k, 0, 1]
                answer[1, k, q] = answer[1, k, q] + (w if q == CUT - 1 else mv(c_maps[k, q + 1 - MID, 1], w))
            if q == MID - 1:
                for kk, qq in b_sent:
                    if qq < MID:
                        b_copy(kk, qq).start()
        for k, q in b_sent:
            if q >= MID:
                b_copy(k, q).start()
        for k, q in a_sent:
            if MID <= q < CUT:
                a_copy(k, q).start()

        @pl.when(base == 0)
        def _():
            for k in range(2):
                a_copy(k, CUT).start()

        in_a[...] = answer[0, 1, MID]
        in_b[...] = answer[1, 1, MID]

    @pl.when(jnp.logical_not(is_mid) & (st != 0))
    def _():
        a_copy(0, 1).wait_recv()

    @pl.when(st == 0)
    def _():
        in_a[...] = jnp.zeros((NC, 4, 128), jnp.float32)

    a_in = in_a[...]

    def side_y_copy(q):
        return pltpu.make_async_remote_copy(
            y_out, side_y.at[pos], sys_sem.at[q], syr_sem.at[pos], **to(base + q, pt)
        )

    @pl.when(left & (pos > 0))
    def _():
        y_out[...] = mv(maps[2], a_in) + vecs[1]
        for q in range(MID - 1):
            @pl.when(pos > q)
            def _():
                side_y_copy(q).start()

    for e in range(1, MID):
        @pl.when(pos < e)
        def _():
            pltpu.make_async_copy(maps.at[1], side_b.at[e], sbr_sem.at[e]).wait()
            pltpu.make_async_copy(y_out, side_y.at[e], syr_sem.at[e]).wait()

    @pl.when(jnp.logical_not(is_mid))
    def _():
        b_copy(0, 0).wait_recv()

    for e in range(MID - 1, 0, -1):
        @pl.when(pos < e)
        def _():
            in_b[...] = mv(side_b[e], in_b[...]) + side_y[e]

    b_in = in_b[...] * jnp.where(st == NS - 1, 0.0, 1.0)

    a1 = jnp.where(is_cut, ghost[...], mv(m0, a_in) + v0)
    b_h0 = (mv(b1, b_in) + mv(w1, a1) + ww1) * keep
    vh[0, :, 0:4, :] = a_in
    vh[0, :, 4:8, :] = a1
    vh[1, :, 0:4, :] = b_h0
    vh[1, :, 4:8, :] = b_in
    a_h, b_h = vh[0], vh[1]
    for i in range(8):
        out[:, pl.ds(i, 8, stride=8), :] = (
            flow_v[:, pl.ds(i, 8, stride=8), :] + c_v[i] + mv(p_v[i], a_h) + mv(q_v[i], b_h)
        )

    @pl.when(((pos > 0) & left) | near)
    def _():
        map_copy(0).wait_send()

    @pl.when(near)
    def _():
        map_copy(1).wait_send()

    @pl.when(near | is_cut)
    def _():
        map_copy(2).wait_send()
        w_copy(centre, pos).wait_send()

    @pl.when(jnp.logical_not(is_mid))
    def _():
        v_copy().wait_send()

    for q in range(MID - 1):
        @pl.when(left & (pos > q))
        def _():
            side_b_copy(q).wait_send()
            side_y_copy(q).wait_send()

    @pl.when(is_mid)
    def _():
        for k, q in a_sent:
            if q < CUT:
                a_copy(k, q).wait_send()

        @pl.when(base == 0)
        def _():
            for k in range(2):
                a_copy(k, CUT).wait_send()

        for k, q in b_sent:
            b_copy(k, q).wait_send()


def to_tiles(x):
    lead = x.shape[:-2]
    x = x.reshape(lead + (2, 8, 4, 128))
    n = len(lead)
    x = jnp.transpose(x, tuple(range(n)) + (n, n + 2, n + 1, n + 3))
    return x.reshape(lead + (64, 128))


def from_tiles(x):
    lead = x.shape[:-2]
    x = x.reshape(lead + (2, 4, 8, 128))
    n = len(lead)
    x = jnp.transpose(x, tuple(range(n)) + (n, n + 2, n + 1, n + 3))
    return x.reshape(lead + (16, 512))


def local(flow_state, residual, spread, diag_inv, lower_jac, upper_jac, partner):
    f32 = jnp.float32
    vm = lambda *s: pltpu.VMEM(s, f32)
    dma = lambda *n: pltpu.SemaphoreType.DMA(n)
    hbm = pl.BlockSpec(memory_space=pltpu.HBM)
    updated = pl.pallas_call(
        kernel,
        out_shape=jax.ShapeDtypeStruct((NC, 64, 128), f32),
        in_specs=[hbm] * 7,
        out_specs=pl.BlockSpec(memory_space=pltpu.VMEM),
        scratch_shapes=[
            vm(5, 64, 128), vm(5, 64, 128), vm(64, 128), vm(25, 64, 128), vm(25, 64, 128), vm(25, 64, 128), vm(5, 64, 128),
            vm(8, 5, 5, 8, 128), vm(8, 5, 5, 8, 128), vm(8, 5, 5, 8, 128), vm(8, 5, 5, 8, 128), vm(8, 5, 5, 8, 128), vm(8, 5, 8, 128),
            vm(5, 2, 8, 128), vm(5, 2, 8, 128), vm(ROW, 5, 4, 128), vm(5, 4, 128), vm(3, 5, 4, 128), vm(4, 5, 4, 128), vm(5, 4, 128),
            vm(3, 5, 5, 4, 128), vm(2, 5, 4, 128), vm(2, 5, 8, 128),
            vm(2, CUT, 3, 5, 5, 4, 128), vm(2, CUT, 2, 5, 4, 128), vm(2, 2, CUT + 1, 5, 4, 128),
            vm(5, 4, 128), vm(5, 4, 128), vm(MID, 5, 5, 4, 128), vm(MID, 5, 4, 128), vm(5, 4, 128),
            pltpu.SMEM((128,), jnp.int32), dma(7), dma(4), dma(4), dma(ROW), dma(ROW), dma(3), dma(3), pltpu.SemaphoreType.REGULAR,
            dma(3), dma(2, CUT, 3), dma(2), dma(2, CUT, 2), dma(MID), dma(MID), dma(MID), dma(MID),
            dma(2, CUT + 1), dma(1), dma(2, CUT + 1), dma(1),
        ],
        compiler_params=pltpu.CompilerParams(
            collective_id=0, has_side_effects=True, vmem_limit_bytes=60 * 1024 * 1024
        ),
        name="lusgs",
    )(
        to_tiles(flow_state), to_tiles(residual), to_tiles(spread), to_tiles(diag_inv),
        to_tiles(lower_jac), to_tiles(upper_jac), partner,
    )
    return from_tiles(updated)


def solution(mesh):
    blocks = P(None, "stream", "pitch")
    in_specs = (blocks, blocks, P("stream", "pitch"), blocks, blocks, blocks, P())
    return jax.shard_map(local, mesh=mesh, in_specs=in_specs, out_specs=blocks, check_vma=False)
```

```python
import jax
import jax.numpy as jnp
from jax import lax
from jax.experimental import pallas as pl
from jax.experimental.pallas import tpu as pltpu
from jax.sharding import PartitionSpec as P

MESH = pl.DeviceIdType.MESH
NC = 5
NS = 16
NPI = 32
CUT = 8
ROW = 8
MID = 6
LEFT = 5
SUB = 3


def mm(a, b):
    return jnp.stack([sum(a[r, k][None] * b[k] for k in range(NC)) for r in range(NC)])


def mv(a, x):
    return sum(a[:, k] * x[k][None] for k in range(NC))


def kernel(
    flow, res, spr, dinv, low, upp, partner, out,
    flow_v, res_v, spr_v, d_v, l_v, u_v, src_v,
    s_v, t_v, f_v, q_v, p_v, c_v,
    halo_lo, halo_hi, rot, rots, chosen, facing, ghost,
    maps, vecs, vh, c_maps, c_vecs, answer, in_a, in_b, side_b, side_y, y_out, hop_in,
    part_s, ld_sem, hs_sem, hr_sem, gs_sem, gr_sem, xs_sem, xr_sem, ready,
    ms_sem, cm_sem, vs_sem, cv_sem, sbs_sem, sbr_sem, sys_sem, syr_sem, as_sem, ar_sem, bs_sem, br_sem, hs2_sem, hr2_sem,
):
    st = lax.axis_index("stream")
    pt = lax.axis_index("pitch")
    up_p, dn_p = lax.rem(pt + 1, NPI), lax.rem(pt + NPI - 1, NPI)
    is_cut = st == CUT
    pos = lax.rem(st, CUT)
    base = st - pos
    core = lax.rem(pt, 2)
    pair = pt - core
    centre = base + MID
    before = lax.rem(st + NS - CUT + MID, NS)
    is_mid = (pos == MID) & (core == 1)
    left = pos < LEFT
    chained = (base == 0) & (pos <= SUB)
    is_sub = (base == 0) & (pos == SUB) & (core == 1)
    home = jnp.where(chained, base + SUB, centre)
    unheard = (base == 0) & (pt == 0)
    near = (pos >= LEFT) & jnp.logical_not(is_mid)
    row = pt // ROW
    row_peers = [row * ROW + lax.rem(pt + d, ROW) for d in range(1, ROW)]
    column_peers = [lax.rem(pt + d * ROW, NPI) for d in range(1, NPI // ROW)]

    def to(stream, pitch):
        return dict(device_id=(stream, pitch), device_id_type=MESH)

    loads = [
        pltpu.make_async_copy(h, v, ld_sem.at[i])
        for i, (h, v) in enumerate(
            ((flow, flow_v), (dinv, d_v), (low, l_v), (upp, u_v), (res, res_v), (spr, spr_v))
        )
    ]

    loads[0].start()
    barrier = pltpu.get_barrier_semaphore()
    for nb in (up_p, dn_p):
        pl.semaphore_signal(barrier, inc=1, **to(st, nb))

    @pl.when(left)
    def _():
        @pl.when((base != 0) | (pos >= SUB))
        def _():
            pl.semaphore_signal(barrier, inc=1, **to(centre, pair + 1))

        for q in range(1, LEFT):
            @pl.when((pos < q) & jnp.logical_not(unheard & (pos == 0)))
            def _():
                pl.semaphore_signal(barrier, inc=1, **to(base + q, pt))

    @pl.when((base == 0) & (pos == LEFT - 1))
    def _():
        pl.semaphore_signal(barrier, inc=1, **to(base + SUB, pair + 1))

    @pl.when(is_sub)
    def _():
        for q in range(SUB + 1):
            for k in range(2):
                if (k, q) != (1, SUB):
                    pl.semaphore_signal(barrier, inc=1, **to(base + q, pair + k))

    @pl.when(is_mid)
    def _():
        for q in range(LEFT, CUT):
            for k in range(2):
                if (q, k) != (MID, 1):
                    pl.semaphore_signal(barrier, inc=1, **to(base + q, pair + k))

        @pl.when(base == 0)
        def _():
            for k in range(2):
                pl.semaphore_signal(barrier, inc=1, **to(CUT, pair + k))

    @pl.when(is_cut)
    def _():
        for nb in row_peers + column_peers:
            pl.semaphore_signal(barrier, inc=1, **to(st, nb))

    for c in loads[1:]:
        c.start()

    expected = (
        2 + jnp.where(is_cut, len(row_peers) + len(column_peers) + 1, 0) + jnp.where(is_mid, jnp.where(base == 0, 2 * (LEFT - SUB), 2 * LEFT), 0)
        + jnp.where(near | (chained & jnp.logical_not(is_sub)), 1, 0) + jnp.where(is_sub, 2, 0)
        + jnp.where(left & (pos > 0), pos - jnp.where(unheard, 1, 0), 0)
    )
    pl.semaphore_wait(barrier, expected)

    @pl.when(is_mid)
    def _():
        for q in range(LEFT):
            for k in range(2):
                @pl.when((base != 0) | (q == LEFT - 1) | ((q == SUB) & (k == 1)))
                def _():
                    pl.semaphore_signal(ready, inc=1, **to(base + q, pair + k))

    loads[0].wait()

    def halos():
        copies = []
        for h in range(2):
            copies.append(
                pltpu.make_async_remote_copy(
                    flow_v.at[:, pl.ds(h * 32 + 24, 8), :], halo_lo.at[:, h],
                    hs_sem.at[h], hr_sem.at[h], **to(st, up_p),
                )
            )
            copies.append(
                pltpu.make_async_remote_copy(
                    flow_v.at[:, pl.ds(h * 32, 8), :], halo_hi.at[:, h],
                    hs_sem.at[2 + h], hr_sem.at[2 + h], **to(st, dn_p),
                )
            )
        return copies

    for c in halos():
        c.start()

    def row_copies():
        return [
            pltpu.make_async_remote_copy(
                rots, rot.at[lax.rem(pt, ROW)], gs_sem.at[d], gr_sem.at[d], **to(st, nb)
            )
            for d, nb in enumerate(row_peers)
        ]

    def column_copies():
        return [
            pltpu.make_async_remote_copy(
                chosen.at[d], facing.at[row], xs_sem.at[d], xr_sem.at[d], **to(st, nb)
            )
            for d, nb in enumerate(column_peers)
        ]

    def choose(target, nb):
        for k in range(4):
            who = part_s[nb * 4 + k]
            target[:, k : k + 1, :] = rot[lax.rem(who // 4, ROW), :, pl.ds(lax.rem(who, 4), 1), :]

    @pl.when(is_cut)
    def _():
        rots[...] = flow_v[:, pl.ds(7, 4, stride=8), :]
        rot[lax.rem(pt, ROW)] = flow_v[:, pl.ds(7, 4, stride=8), :]
        pltpu.make_async_copy(partner, part_s, ld_sem.at[6]).start()
        for c in row_copies():
            c.start()

    for c in loads[1:4]:
        c.wait()

    def block(ref, i):
        return ref[:, pl.ds(i, 8, stride=8), :].reshape(NC, NC, 8, 128)

    def first(i, f):
        s = mm(block(d_v, i), block(l_v, i))
        s_v[i] = s
        f = jnp.where(i == 0, s, mm(s, f))
        f_v[i] = f
        return f

    lax.fori_loop(0, 8, lambda i, _: (first(i, f_v[jnp.maximum(i - 1, 0)]), 0)[1], 0)

    keep = jnp.where(is_cut, 0.0, 1.0)
    m0, m1 = f_v[7, :, :, 0:4, :], f_v[7, :, :, 4:8, :]
    maps[0] = mm(m1, m0)

    def map_copy(k, stream=home):
        slot = pos
        return pltpu.make_async_remote_copy(
            maps.at[k], c_maps.at[core, slot, k], ms_sem.at[k], cm_sem.at[core, slot, k], **to(stream, pair + 1)
        )

    @pl.when(near | (chained & jnp.logical_not(is_sub) & (pos > 0)))
    def _():
        map_copy(0).start()

    def last(j, _):
        i = 7 - j
        n = jnp.minimum(i + 1, 7)
        t = mm(block(d_v, i), block(u_v, i))
        t_v[i] = t
        q_v[i] = jnp.where(i == 7, t, mm(t, q_v[n]))
        p_v[i] = f_v[i] + jnp.where(i == 7, 0.0, mm(t, p_v[n]))
        return 0

    lax.fori_loop(0, 8, last, 0)

    b0, b1 = q_v[0, :, :, 0:4, :], q_v[0, :, :, 4:8, :]
    maps[1] = mm(b0, b1)
    w0, w1 = p_v[0, :, :, 0:4, :], p_v[0, :, :, 4:8, :]
    maps[2] = w0 + mm(b0, mm(w1, m0)) * keep

    def side_b_copy(q):
        return pltpu.make_async_remote_copy(
            maps.at[1], side_b.at[pos], sbs_sem.at[q], sbr_sem.at[pos], **to(base + q, pt)
        )

    @pl.when(near)
    def _():
        map_copy(1).start()
        map_copy(2).start()

    @pl.when(is_cut)
    def _():
        map_copy(2, before).start()

    for q in range(LEFT - 1):
        @pl.when(left & (pos > q) & ((q > 0) | jnp.logical_not(unheard)))
        def _():
            side_b_copy(q).start()

    for c in loads[4:]:
        c.wait()
    for c in halos():
        c.wait()

    for h in range(2):
        for c in range(4):
            r = h * 32 + c * 8
            mid = flow_v[:, r : r + 8, :]
            lo = halo_lo[:, h] if c == 0 else flow_v[:, r - 8 : r, :]
            hi = halo_hi[:, h] if c == 3 else flow_v[:, r + 8 : r + 16, :]
            src_v[:, r : r + 8, :] = res_v[:, r : r + 8, :] + spr_v[r : r + 8, :][None] * (
                hi + lo - 2.0 * mid
            )

    star = None
    for i in range(8):
        now = mv(block(d_v, i), src_v[:, pl.ds(i, 8, stride=8), :])
        star = now if star is None else now + mv(s_v[i], star)
        c_v[i] = star
    vh[0] = star
    v0, v1 = vh[0, :, 0:4, :], vh[0, :, 4:8, :]
    ghost[...] = v0

    def v_copy():
        return pltpu.make_async_remote_copy(
            vecs.at[0], c_vecs.at[core, pos, 0], vs_sem.at[0], cv_sem.at[core, pos, 0], **to(home, pair + 1)
        )

    def w_copy(stream, slot):
        return pltpu.make_async_remote_copy(
            vecs.at[1], c_vecs.at[core, slot, 1], vs_sem.at[1], cv_sem.at[core, slot, 1], **to(stream, pair + 1)
        )

    @pl.when(jnp.logical_not(is_cut))
    def _():
        vecs[0] = mv(m1, v0) + v1

        @pl.when(near)
        def _():
            v_copy().start()

    ch = star
    for i in range(6, -1, -1):
        ch = c_v[i] + mv(t_v[i], ch)
        c_v[i] = ch
    vh[1] = ch
    ww0, ww1 = vh[1, :, 0:4, :], vh[1, :, 4:8, :]
    vecs[1] = ww0 + mv(b0, mv(w1, v0) + ww1) * keep

    @pl.when(near)
    def _():
        w_copy(centre, pos).start()

    @pl.when(is_cut)
    def _():
        w_copy(before, 0).start()

    @pl.when(left & jnp.logical_not(is_cut) & jnp.logical_not(is_sub))
    def _():
        @pl.when(jnp.logical_not(chained))
        def _():
            pl.semaphore_wait(ready, 1)

        v_copy().start()

        @pl.when((pos > 0) & jnp.logical_not(chained))
        def _():
            map_copy(0).start()

    @pl.when(is_cut)
    def _():
        pltpu.make_async_copy(partner, part_s, ld_sem.at[6]).wait()
        for c in row_copies():
            c.wait()
        choose(facing.at[row], pt)
        for d, c in enumerate(column_copies()):
            choose(chosen.at[d], column_peers[d])
            c.start()

    @pl.when(is_cut)
    def _():
        for c in column_copies():
            c.wait()
        for k in range(4):
            who = part_s[pt * 4 + k]
            ghost[:, k : k + 1, :] = facing[who // (4 * ROW), :, pl.ds(k, 1), :]
        vecs[0] = mv(m1, ghost[...]) + v1
        pl.semaphore_wait(ready, 1)
        v_copy().start()

    def a_copy(k, q):
        return pltpu.make_async_remote_copy(
            answer.at[0, k, q], in_a, as_sem.at[k, q], ar_sem.at[0], **to(lax.rem(base + q, NS), pair + k)
        )

    def b_copy(k, q):
        return pltpu.make_async_remote_copy(
            answer.at[1, k, max(q, LEFT - 1)], in_b, bs_sem.at[k, q], br_sem.at[0], **to(base + q, pair + k)
        )

    def arrived_map(k, q, m):
        pltpu.make_async_copy(maps.at[m], c_maps.at[k, q, m], cm_sem.at[k, q, m]).wait()

    def arrived_vec(k, q, m):
        pltpu.make_async_copy(vecs.at[m], c_vecs.at[k, q, m], cv_sem.at[k, q, m]).wait()

    def hop_copy(k):
        return pltpu.make_async_remote_copy(
            answer.at[0, k, SUB + 1], hop_in.at[k], hs2_sem.at[k], hr2_sem.at[k], **to(centre, pt)
        )

    a_sent = [(k, q) for q in range(1, CUT + 1) for k in range(2) if (k, q) != (1, MID)]
    b_sent = [(k, q) for q in range(CUT) for k in range(2) if (k, q) != (1, MID)]

    @pl.when(is_sub)
    def _():
        c_maps[1, SUB, 0] = maps[0]
        c_vecs[1, SUB, 0] = vecs[0]
        for k in (1, 0):
            for q in range(SUB + 1):
                if (k, q) != (1, SUB):
                    if q:
                        arrived_map(k, q, 0)
                    arrived_vec(k, q, 0)
            hop = c_vecs[k, 0, 0]
            for q in range(1, SUB + 2):
                answer[0, k, q] = hop
                if q <= SUB:
                    hop = mv(c_maps[k, q, 0], hop) + c_vecs[k, q, 0]
            for q in range(SUB + 1, 0, -1):
                if (k, q) != (1, SUB):
                    a_copy(k, q).start()
            if k == 1:
                in_a[...] = answer[0, 1, SUB]
                pl.semaphore_wait(ready, 1)
            hop_copy(k).start()

    @pl.when(is_mid)
    def _():
        c_maps[1, MID] = maps[...]
        c_vecs[1, MID] = vecs[...]
        for k in (1, 0):
            @pl.when(base == 0)
            def _():
                hop_copy(k).wait_recv()
                answer[0, k, LEFT - 1] = hop_in[k]

            @pl.when(base != 0)
            def _():
                for q in range(LEFT - 1):
                    if q:
                        arrived_map(k, q, 0)
                    arrived_vec(k, q, 0)
                early = c_vecs[k, 0, 0]
                for q in range(1, LEFT):
                    answer[0, k, q] = early
                    a_copy(k, q).start()
                    if q < LEFT - 1:
                        early = mv(c_maps[k, q, 0], early) + c_vecs[k, q, 0]

            arrived_map(k, LEFT - 1, 0)
            arrived_vec(k, LEFT - 1, 0)
            a = mv(c_maps[k, LEFT - 1, 0], answer[0, k, LEFT - 1]) + c_vecs[k, LEFT - 1, 0]
            answer[0, k, LEFT] = a
            for q in range(LEFT, CUT):
                if (k, q) != (1, MID):
                    for m in range(3):
                        arrived_map(k, q, m)
                    for m in range(2):
                        arrived_vec(k, q, m)

            @pl.when(base == 0)
            def _():
                arrived_map(k, 0, 2)

            @pl.when(base != 0)
            def _():
                c_maps[k, 0, 2] = jnp.zeros((NC, NC, 4, 128), jnp.float32)
                c_vecs[k, 0, 1] = jnp.zeros((NC, 4, 128), jnp.float32)

            for q in range(LEFT, CUT):
                a = mv(c_maps[k, q, 0], a) + c_vecs[k, q, 0]
                answer[0, k, q + 1] = a
            b = mv(c_maps[k, 0, 2], a)
            answer[1, k, CUT - 1] = b
            for q in range(CUT - 1, LEFT - 1, -1):
                b = mv(c_maps[k, q, 1], b) + mv(c_maps[k, q, 2], answer[0, k, q]) + c_vecs[k, q, 1]
                answer[1, k, q - 1] = b
                c_maps[k, q - LEFT, 1] = c_maps[k, q, 1] if q == CUT - 1 else mm(c_maps[k, q, 1], c_maps[k, q + 1 - LEFT, 1])

            @pl.when(base == 0)
            def _():
                arrived_vec(k, 0, 1)

            w = c_vecs[k, 0, 1]
            for q in range(LEFT - 1, CUT):
                answer[1, k, q] = answer[1, k, q] + (w if q == CUT - 1 else mv(c_maps[k, q + 1 - LEFT, 1], w))
                if q == LEFT - 1:
                    for j in range(LEFT):
                        b_copy(k, j).start()
                elif (k, q) != (1, MID):
                    b_copy(k, q).start()
            for q in range(LEFT, CUT):
                if (k, q) != (1, MID):
                    a_copy(k, q).start()

            @pl.when(base == 0)
            def _():
                a_copy(k, CUT).start()

            if k == 1:
                in_a[...] = answer[0, 1, MID]
                in_b[...] = answer[1, 1, MID]

    @pl.when(jnp.logical_not(is_mid | is_sub) & (st != 0))
    def _():
        a_copy(0, 1).wait_recv()

    @pl.when(st == 0)
    def _():
        in_a[...] = jnp.zeros((NC, 4, 128), jnp.float32)

    a_in = in_a[...]

    def side_y_copy(q):
        return pltpu.make_async_remote_copy(
            y_out, side_y.at[pos], sys_sem.at[q], syr_sem.at[pos], **to(base + q, pt)
        )

    @pl.when(left & (pos > 0))
    def _():
        @pl.when(unheard)
        def _():
            side_b_copy(0).start()

        y_out[...] = mv(maps[2], a_in) + vecs[1]
        for q in range(LEFT - 1):
            @pl.when(pos > q)
            def _():
                side_y_copy(q).start()

    for e in range(1, LEFT):
        @pl.when(pos < e)
        def _():
            pltpu.make_async_copy(maps.at[1], side_b.at[e], sbr_sem.at[e]).wait()
            pltpu.make_async_copy(y_out, side_y.at[e], syr_sem.at[e]).wait()

    @pl.when(jnp.logical_not(is_mid))
    def _():
        b_copy(0, 0).wait_recv()

    for e in range(LEFT - 1, 0, -1):
        @pl.when(pos < e)
        def _():
            in_b[...] = mv(side_b[e], in_b[...]) + side_y[e]

    b_in = in_b[...] * jnp.where(st == NS - 1, 0.0, 1.0)

    a1 = jnp.where(is_cut, ghost[...], mv(m0, a_in) + v0)
    b_h0 = (mv(b1, b_in) + mv(w1, a1) + ww1) * keep
    vh[0, :, 0:4, :] = a_in
    vh[0, :, 4:8, :] = a1
    vh[1, :, 0:4, :] = b_h0
    vh[1, :, 4:8, :] = b_in
    a_h, b_h = vh[0], vh[1]
    for i in range(8):
        out[:, pl.ds(i, 8, stride=8), :] = (
            flow_v[:, pl.ds(i, 8, stride=8), :] + c_v[i] + mv(p_v[i], a_h) + mv(q_v[i], b_h)
        )

    @pl.when(((pos > 0) & left & jnp.logical_not(is_sub)) | near)
    def _():
        map_copy(0).wait_send()

    @pl.when(is_sub)
    def _():
        for k in range(2):
            hop_copy(k).wait_send()
            for q in range(1, SUB + 2):
                if (k, q) != (1, SUB):
                    a_copy(k, q).wait_send()

    @pl.when(near)
    def _():
        map_copy(1).wait_send()

    @pl.when(near | is_cut)
    def _():
        map_copy(2).wait_send()
        w_copy(centre, pos).wait_send()

    @pl.when(jnp.logical_not(is_mid | is_sub))
    def _():
        v_copy().wait_send()

    for q in range(LEFT - 1):
        @pl.when(left & (pos > q))
        def _():
            side_b_copy(q).wait_send()
            side_y_copy(q).wait_send()

    @pl.when(is_mid)
    def _():
        for k, q in a_sent:
            if LEFT <= q < CUT:
                a_copy(k, q).wait_send()

        @pl.when(base != 0)
        def _():
            for k, q in a_sent:
                if q < LEFT:
                    a_copy(k, q).wait_send()

        @pl.when(base == 0)
        def _():
            for k in range(2):
                a_copy(k, CUT).wait_send()

        for k, q in b_sent:
            b_copy(k, q).wait_send()


def to_tiles(x):
    lead = x.shape[:-2]
    x = x.reshape(lead + (2, 8, 4, 128))
    n = len(lead)
    x = jnp.transpose(x, tuple(range(n)) + (n, n + 2, n + 1, n + 3))
    return x.reshape(lead + (64, 128))


def from_tiles(x):
    lead = x.shape[:-2]
    x = x.reshape(lead + (2, 4, 8, 128))
    n = len(lead)
    x = jnp.transpose(x, tuple(range(n)) + (n, n + 2, n + 1, n + 3))
    return x.reshape(lead + (16, 512))


def local(flow_state, residual, spread, diag_inv, lower_jac, upper_jac, partner):
    f32 = jnp.float32
    vm = lambda *s: pltpu.VMEM(s, f32)
    dma = lambda *n: pltpu.SemaphoreType.DMA(n)
    hbm = pl.BlockSpec(memory_space=pltpu.HBM)
    updated = pl.pallas_call(
        kernel,
        out_shape=jax.ShapeDtypeStruct((NC, 64, 128), f32),
        in_specs=[hbm] * 7,
        out_specs=pl.BlockSpec(memory_space=pltpu.VMEM),
        scratch_shapes=[
            vm(5, 64, 128), vm(5, 64, 128), vm(64, 128), vm(25, 64, 128), vm(25, 64, 128), vm(25, 64, 128), vm(5, 64, 128),
            vm(8, 5, 5, 8, 128), vm(8, 5, 5, 8, 128), vm(8, 5, 5, 8, 128), vm(8, 5, 5, 8, 128), vm(8, 5, 5, 8, 128), vm(8, 5, 8, 128),
            vm(5, 2, 8, 128), vm(5, 2, 8, 128), vm(ROW, 5, 4, 128), vm(5, 4, 128), vm(3, 5, 4, 128), vm(4, 5, 4, 128), vm(5, 4, 128),
            vm(3, 5, 5, 4, 128), vm(2, 5, 4, 128), vm(2, 5, 8, 128),
            vm(2, CUT, 3, 5, 5, 4, 128), vm(2, CUT, 2, 5, 4, 128), vm(2, 2, CUT + 1, 5, 4, 128),
            vm(5, 4, 128), vm(5, 4, 128), vm(LEFT, 5, 5, 4, 128), vm(LEFT, 5, 4, 128), vm(5, 4, 128), vm(2, 5, 4, 128),
            pltpu.SMEM((128,), jnp.int32), dma(7), dma(4), dma(4), dma(ROW), dma(ROW), dma(3), dma(3), pltpu.SemaphoreType.REGULAR,
            dma(3), dma(2, CUT, 3), dma(2), dma(2, CUT, 2), dma(LEFT), dma(LEFT), dma(LEFT), dma(LEFT),
            dma(2, CUT + 1), dma(1), dma(2, CUT + 1), dma(1), dma(2), dma(2),
        ],
        compiler_params=pltpu.CompilerParams(
            collective_id=0, has_side_effects=True, vmem_limit_bytes=60 * 1024 * 1024
        ),
        name="lusgs",
    )(
        to_tiles(flow_state), to_tiles(residual), to_tiles(spread), to_tiles(diag_inv),
        to_tiles(lower_jac), to_tiles(upper_jac), partner,
    )
    return from_tiles(updated)


def solution(mesh):
    blocks = P(None, "stream", "pitch")
    in_specs = (blocks, blocks, P("stream", "pitch"), blocks, blocks, blocks, P())
    return jax.shard_map(local, mesh=mesh, in_specs=in_specs, out_specs=blocks, check_vma=False)
```

```python
import jax
import jax.numpy as jnp
from jax import lax
from jax.experimental import pallas as pl
from jax.experimental.pallas import tpu as pltpu
from jax.sharding import PartitionSpec as P

MESH = pl.DeviceIdType.MESH
NC = 5
NS = 16
NPI = 32
CUT = 8
ROW = 8
MID = 6
LEFT = 5
SUB = 3


def mm(a, b):
    return jnp.stack([sum(a[r, k][None] * b[k] for k in range(NC)) for r in range(NC)])


def mv(a, x):
    return sum(a[:, k] * x[k][None] for k in range(NC))


def kernel(
    flow, res, spr, dinv, low, upp, partner, out,
    out_0, out_1, out_2, out_3, out_4, out_sem, flow_v, res_v, spr_v, d_v, l_v, u_v, src_v,
    s_v, t_v, f_v, q_v, p_v, c_v,
    halo_lo, halo_hi, rot, rots, chosen, facing, ghost,
    maps, vecs, vh, c_maps, c_vecs, answer, in_a, in_b, side_b, side_y, y_out, hop_in,
    part_s, ld_sem, hs_sem, hr_sem, gs_sem, gr_sem, xs_sem, xr_sem, ready, here,
    ms_sem, cm_sem, vs_sem, cv_sem, sbs_sem, sbr_sem, sys_sem, syr_sem, as_sem, ar_sem, bs_sem, br_sem, hs2_sem, hr2_sem,
):
    outs = (out_0, out_1, out_2, out_3, out_4)
    st = lax.axis_index("stream")
    pt = lax.axis_index("pitch")
    up_p, dn_p = lax.rem(pt + 1, NPI), lax.rem(pt + NPI - 1, NPI)
    is_cut = st == CUT
    pos = lax.rem(st, CUT)
    base = st - pos
    core = lax.rem(pt, 2)
    pair = pt - core
    centre = base + MID
    before = lax.rem(st + NS - CUT + MID, NS)
    is_mid = (pos == MID) & (core == 1)
    left = pos < LEFT
    chained = pos <= SUB
    is_sub = (pos == SUB) & (core == 1)
    home = jnp.where(chained, base + SUB, centre)
    unheard = (base == 0) & (pt == 0)
    near = (pos >= LEFT) & jnp.logical_not(is_mid)
    row = pt // ROW
    row_peers = [row * ROW + lax.rem(pt + d, ROW) for d in range(1, ROW)]
    column_peers = [lax.rem(pt + d * ROW, NPI) for d in range(1, NPI // ROW)]

    def to(stream, pitch):
        return dict(device_id=(stream, pitch), device_id_type=MESH)

    loads = [
        pltpu.make_async_copy(h, v, ld_sem.at[i])
        for i, (h, v) in enumerate(
            ((flow, flow_v), (dinv, d_v), (low, l_v), (upp, u_v), (res, res_v), (spr, spr_v))
        )
    ]

    loads[0].start()
    barrier = pltpu.get_barrier_semaphore()
    for nb in (up_p, dn_p):
        pl.semaphore_signal(barrier, inc=1, **to(st, nb))

    @pl.when(left)
    def _():
        @pl.when(pos >= SUB)
        def _():
            pl.semaphore_signal(barrier, inc=1, **to(centre, pair + 1))

        for q in range(1, LEFT):
            @pl.when((pos < q) & jnp.logical_not(unheard & (pos == 0)))
            def _():
                pl.semaphore_signal(barrier, inc=1, **to(base + q, pt))

    @pl.when(pos == LEFT - 1)
    def _():
        pl.semaphore_signal(barrier, inc=1, **to(base + SUB, pair + 1))

    @pl.when(is_sub)
    def _():
        for q in range(SUB + 1):
            for k in range(2):
                if (k, q) != (1, SUB):
                    pl.semaphore_signal(barrier, inc=1, **to(base + q, pair + k))

    @pl.when(is_mid)
    def _():
        for q in range(LEFT, CUT):
            for k in range(2):
                if (q, k) != (MID, 1):
                    pl.semaphore_signal(barrier, inc=1, **to(base + q, pair + k))

        @pl.when(base == 0)
        def _():
            for k in range(2):
                pl.semaphore_signal(barrier, inc=1, **to(CUT, pair + k))

    @pl.when(is_cut)
    def _():
        for nb in row_peers + column_peers:
            @pl.when(nb > pt)
            def _():
                pl.semaphore_signal(barrier, inc=1, **to(st, nb))

    for c in loads[1:]:
        c.start()

    expected = (
        2 + jnp.where(is_cut, pt - row * ROW + row + 1, 0) + jnp.where(is_mid, 2 * (LEFT - SUB), 0)
        + jnp.where(near | (chained & jnp.logical_not(is_sub)), 1, 0) + jnp.where(is_sub, 2, 0)
        + jnp.where(left & (pos > 0), pos - jnp.where(unheard, 1, 0), 0)
    )
    pl.semaphore_wait(barrier, expected)

    @pl.when(is_mid)
    def _():
        for q, k in ((LEFT - 1, 0), (LEFT - 1, 1), (SUB, 1)):
            pl.semaphore_signal(ready, inc=1, **to(base + q, pair + k))

    @pl.when(is_cut)
    def _():
        for nb in row_peers + column_peers:
            @pl.when(nb < pt)
            def _():
                pl.semaphore_signal(here, inc=1, **to(st, nb))

    loads[0].wait()

    def halos():
        copies = []
        for h in range(2):
            copies.append(
                pltpu.make_async_remote_copy(
                    flow_v.at[:, pl.ds(h * 32 + 24, 8), :], halo_lo.at[:, h],
                    hs_sem.at[h], hr_sem.at[h], **to(st, up_p),
                )
            )
            copies.append(
                pltpu.make_async_remote_copy(
                    flow_v.at[:, pl.ds(h * 32, 8), :], halo_hi.at[:, h],
                    hs_sem.at[2 + h], hr_sem.at[2 + h], **to(st, dn_p),
                )
            )
        return copies

    for c in halos():
        c.start()

    def row_copies():
        return [
            pltpu.make_async_remote_copy(
                rots, rot.at[lax.rem(pt, ROW)], gs_sem.at[d], gr_sem.at[d], **to(st, nb)
            )
            for d, nb in enumerate(row_peers)
        ]

    def column_copies():
        return [
            pltpu.make_async_remote_copy(
                chosen.at[d], facing.at[row], xs_sem.at[d], xr_sem.at[d], **to(st, nb)
            )
            for d, nb in enumerate(column_peers)
        ]

    def choose(target, nb):
        for k in range(4):
            who = part_s[nb * 4 + k]
            target[:, k : k + 1, :] = rot[lax.rem(who // 4, ROW), :, pl.ds(lax.rem(who, 4), 1), :]

    for c in loads[1:4]:
        c.wait()

    def block(ref, i):
        return ref[:, pl.ds(i, 8, stride=8), :].reshape(NC, NC, 8, 128)

    def first(i, f):
        s = mm(block(d_v, i), block(l_v, i))
        s_v[i] = s
        f = jnp.where(i == 0, s, mm(s, f))
        f_v[i] = f
        return f

    lax.fori_loop(0, 8, lambda i, _: (first(i, f_v[jnp.maximum(i - 1, 0)]), 0)[1], 0)

    keep = jnp.where(is_cut, 0.0, 1.0)
    m0, m1 = f_v[7, :, :, 0:4, :], f_v[7, :, :, 4:8, :]
    maps[0] = mm(m1, m0)

    @pl.when(is_cut)
    def _():
        rots[...] = flow_v[:, pl.ds(7, 4, stride=8), :]
        rot[lax.rem(pt, ROW)] = flow_v[:, pl.ds(7, 4, stride=8), :]
        pltpu.make_async_copy(partner, part_s, ld_sem.at[6]).start()
        higher = len(row_peers) + len(column_peers) - (pt - row * ROW) - row

        @pl.when(higher > 0)
        def _():
            pl.semaphore_wait(here, higher)

        for c in row_copies():
            c.start()

    def map_copy(k, stream=home):
        slot = pos
        return pltpu.make_async_remote_copy(
            maps.at[k], c_maps.at[core, slot, k], ms_sem.at[k], cm_sem.at[core, slot, k], **to(stream, pair + 1)
        )

    @pl.when(near | (chained & jnp.logical_not(is_sub) & (pos > 0)))
    def _():
        map_copy(0).start()

    def last(j, _):
        i = 7 - j
        n = jnp.minimum(i + 1, 7)
        t = mm(block(d_v, i), block(u_v, i))
        t_v[i] = t
        q_v[i] = jnp.where(i == 7, t, mm(t, q_v[n]))
        p_v[i] = f_v[i] + jnp.where(i == 7, 0.0, mm(t, p_v[n]))
        return 0

    lax.fori_loop(0, 8, last, 0)

    b0, b1 = q_v[0, :, :, 0:4, :], q_v[0, :, :, 4:8, :]
    maps[1] = mm(b0, b1)
    w0, w1 = p_v[0, :, :, 0:4, :], p_v[0, :, :, 4:8, :]
    maps[2] = w0 + mm(b0, mm(w1, m0)) * keep

    def side_b_copy(q):
        return pltpu.make_async_remote_copy(
            maps.at[1], side_b.at[pos], sbs_sem.at[q], sbr_sem.at[pos], **to(base + q, pt)
        )

    @pl.when(near)
    def _():
        map_copy(1).start()
        map_copy(2).start()

    @pl.when(is_cut)
    def _():
        map_copy(2, before).start()

    for q in range(LEFT - 1):
        @pl.when(left & (pos > q) & ((q > 0) | jnp.logical_not(unheard)))
        def _():
            side_b_copy(q).start()

    for c in loads[4:]:
        c.wait()
    for c in halos():
        c.wait()

    for h in range(2):
        for c in range(4):
            r = h * 32 + c * 8
            mid = flow_v[:, r : r + 8, :]
            lo = halo_lo[:, h] if c == 0 else flow_v[:, r - 8 : r, :]
            hi = halo_hi[:, h] if c == 3 else flow_v[:, r + 8 : r + 16, :]
            src_v[:, r : r + 8, :] = res_v[:, r : r + 8, :] + spr_v[r : r + 8, :][None] * (
                hi + lo - 2.0 * mid
            )

    star = None
    for i in range(8):
        now = mv(block(d_v, i), src_v[:, pl.ds(i, 8, stride=8), :])
        star = now if star is None else now + mv(s_v[i], star)
        c_v[i] = star
    vh[0] = star
    v0, v1 = vh[0, :, 0:4, :], vh[0, :, 4:8, :]
    ghost[...] = v0

    def v_copy():
        return pltpu.make_async_remote_copy(
            vecs.at[0], c_vecs.at[core, pos, 0], vs_sem.at[0], cv_sem.at[core, pos, 0], **to(home, pair + 1)
        )

    def w_copy(stream, slot):
        return pltpu.make_async_remote_copy(
            vecs.at[1], c_vecs.at[core, slot, 1], vs_sem.at[1], cv_sem.at[core, slot, 1], **to(stream, pair + 1)
        )

    @pl.when(jnp.logical_not(is_cut))
    def _():
        vecs[0] = mv(m1, v0) + v1

        @pl.when(near)
        def _():
            v_copy().start()

    ch = star
    for i in range(6, -1, -1):
        ch = c_v[i] + mv(t_v[i], ch)
        c_v[i] = ch
    vh[1] = ch
    ww0, ww1 = vh[1, :, 0:4, :], vh[1, :, 4:8, :]
    vecs[1] = ww0 + mv(b0, mv(w1, v0) + ww1) * keep

    @pl.when(near)
    def _():
        w_copy(centre, pos).start()

    @pl.when(is_cut)
    def _():
        w_copy(before, 0).start()

    @pl.when(left & jnp.logical_not(is_cut) & jnp.logical_not(is_sub))
    def _():
        @pl.when(jnp.logical_not(chained))
        def _():
            pl.semaphore_wait(ready, 1)

        v_copy().start()

        @pl.when((pos > 0) & jnp.logical_not(chained))
        def _():
            map_copy(0).start()

    @pl.when(is_cut)
    def _():
        pltpu.make_async_copy(partner, part_s, ld_sem.at[6]).wait()
        for c in row_copies():
            c.wait()
        choose(facing.at[row], pt)
        for d, c in enumerate(column_copies()):
            choose(chosen.at[d], column_peers[d])
            c.start()

    @pl.when(is_cut)
    def _():
        for c in column_copies():
            c.wait()
        for k in range(4):
            who = part_s[pt * 4 + k]
            ghost[:, k : k + 1, :] = facing[who // (4 * ROW), :, pl.ds(k, 1), :]
        vecs[0] = mv(m1, ghost[...]) + v1
        v_copy().start()

    def a_copy(k, q):
        return pltpu.make_async_remote_copy(
            answer.at[0, k, q], in_a, as_sem.at[k, q], ar_sem.at[0], **to(lax.rem(base + q, NS), pair + k)
        )

    def b_copy(k, q):
        return pltpu.make_async_remote_copy(
            answer.at[1, k, max(q, LEFT - 1)], in_b, bs_sem.at[k, q], br_sem.at[0], **to(base + q, pair + k)
        )

    def arrived_map(k, q, m):
        pltpu.make_async_copy(maps.at[m], c_maps.at[k, q, m], cm_sem.at[k, q, m]).wait()

    def arrived_vec(k, q, m):
        pltpu.make_async_copy(vecs.at[m], c_vecs.at[k, q, m], cv_sem.at[k, q, m]).wait()

    def hop_copy(k):
        return pltpu.make_async_remote_copy(
            answer.at[0, k, SUB + 1], hop_in.at[k], hs2_sem.at[k], hr2_sem.at[k], **to(centre, pt)
        )

    a_sent = [(k, q) for q in range(1, CUT + 1) for k in range(2) if (k, q) != (1, MID)]
    b_sent = [(k, q) for q in range(CUT) for k in range(2) if (k, q) != (1, MID)]

    @pl.when(is_sub)
    def _():
        c_maps[1, SUB, 0] = maps[0]
        c_vecs[1, SUB, 0] = vecs[0]
        def early(k):
            for q in range(SUB + 1):
                if (k, q) != (1, SUB):
                    if q:
                        arrived_map(k, q, 0)
                    arrived_vec(k, q, 0)
            hop = c_vecs[k, 0, 0]
            for q in range(1, SUB + 2):
                answer[0, k, q] = hop
                if q <= SUB:
                    hop = mv(c_maps[k, q, 0], hop) + c_vecs[k, q, 0]

        def tell(k):
            hop_copy(k).start()
            for q in range(SUB + 1, 0, -1):
                if (k, q) != (1, SUB):
                    a_copy(k, q).start()
            if k == 1:
                in_a[...] = answer[0, 1, SUB]

        @pl.when(base == 0)
        def _():
            early(1)
            for q in range(SUB + 1, 0, -1):
                if q != SUB:
                    a_copy(1, q).start()
            in_a[...] = answer[0, 1, SUB]
            pl.semaphore_wait(ready, 1)
            hop_copy(1).start()
            early(0)
            tell(0)

        @pl.when(base != 0)
        def _():
            pl.semaphore_wait(ready, 1)
            early(0)
            early(1)
            tell(0)
            tell(1)

    def arrived_right(k):
        arrived_map(k, LEFT - 1, 0)
        arrived_vec(k, LEFT - 1, 0)
        for q in range(LEFT, CUT):
            if (k, q) != (1, MID):
                for m in range(3):
                    arrived_map(k, q, m)
                for m in range(2):
                    arrived_vec(k, q, m)
        for q in range(CUT - 2, LEFT - 1, -1):
            c_maps[k, q - LEFT, 1] = mm(c_maps[k, q, 1], c_maps[k, q + 1, 1] if q == CUT - 2 else c_maps[k, q + 1 - LEFT, 1])

        @pl.when(base == 0)
        def _():
            arrived_map(k, 0, 2)

        @pl.when(base != 0)
        def _():
            c_maps[k, 0, 2] = jnp.zeros((NC, NC, 4, 128), jnp.float32)
            c_vecs[k, 0, 1] = jnp.zeros((NC, 4, 128), jnp.float32)

    def right_values(k, a, stop):
        for q in range(LEFT, CUT):
            answer[0, k, q] = a
            a = mv(c_maps[k, q, 0], a) + c_vecs[k, q, 0]
        answer[0, k, CUT] = a
        b = mv(c_maps[k, 0, 2], a)
        answer[1, k, CUT - 1] = b
        for q in range(CUT - 1, stop, -1):
            b = mv(c_maps[k, q, 1], b) + mv(c_maps[k, q, 2], answer[0, k, q]) + c_vecs[k, q, 1]
            answer[1, k, q - 1] = b

    def heard(k):
        hop_copy(k).wait_recv()
        answer[0, k, LEFT - 1] = hop_in[k]
        return mv(c_maps[k, LEFT - 1, 0], hop_in[k]) + c_vecs[k, LEFT - 1, 0]

    def solve(k):
        arrived_right(k)
        a = heard(k)
        right_values(k, a, LEFT - 1)

    def prepare(k):
        arrived_right(k)
        back = c_maps[k, 0, 2]
        for q in range(CUT - 1, LEFT - 1, -1):
            back = c_maps[k, q, 2] + mm(c_maps[k, q, 1], mm(back, c_maps[k, q, 0]))
        c_maps[k, LEFT - 2, 1] = mm(back, c_maps[k, LEFT - 1, 0])
        right_values(k, c_vecs[k, LEFT - 1, 0], LEFT - 1)

    def finish(k, late):
        if late:
            hop_copy(k).wait_recv()
            answer[1, k, LEFT - 1] = answer[1, k, LEFT - 1] + mv(c_maps[k, LEFT - 2, 1], hop_in[k])

        @pl.when(base == 0)
        def _():
            arrived_vec(k, 0, 1)

        w = c_vecs[k, 0, 1]
        answer[1, k, LEFT - 1] = answer[1, k, LEFT - 1] + mv(c_maps[k, 0, 1], w)
        b_copy(k, 0).start()

    def finish_left(cores):
        for j in range(1, LEFT):
            for k in cores:
                b_copy(k, j).start()

    def finish_right(k, late):
        if late:
            right_values(k, mv(c_maps[k, LEFT - 1, 0], hop_in[k]) + c_vecs[k, LEFT - 1, 0], LEFT)
        w = c_vecs[k, 0, 1]
        for q in range(LEFT, CUT):
            if q == CUT - 1:
                more = w
            else:
                more = mv(c_maps[k, CUT - 1, 1] if q == CUT - 2 else c_maps[k, q + 1 - LEFT, 1], w)
            answer[1, k, q] = answer[1, k, q] + more
            if (k, q) != (1, MID):
                b_copy(k, q).start()
                a_copy(k, q).start()

        @pl.when(base == 0)
        def _():
            a_copy(k, CUT).start()

        if k == 1:
            in_a[...] = answer[0, 1, MID]
            in_b[...] = answer[1, 1, MID]

    @pl.when(is_mid)
    def _():
        c_maps[1, MID] = maps[...]
        c_vecs[1, MID] = vecs[...]

        @pl.when(base != 0)
        def _():
            prepare(1)
            prepare(0)
            finish(0, True)
            finish(1, True)
            finish_left((0, 1))
            finish_right(0, True)
            finish_right(1, True)

        @pl.when((base == 0) & (pair == 0))
        def _():
            solve(1)
            finish(1, False)
            finish_left((1,))
            prepare(0)
            finish(0, True)
            finish_left((0,))
            finish_right(1, False)
            finish_right(0, True)

        @pl.when((base == 0) & (pair != 0))
        def _():
            solve(1)
            solve(0)
            finish(0, False)
            finish(1, False)
            finish_left((0, 1))
            finish_right(0, False)
            finish_right(1, False)

    @pl.when(jnp.logical_not(is_mid | is_sub) & (st != 0))
    def _():
        a_copy(0, 1).wait_recv()

    @pl.when(st == 0)
    def _():
        in_a[...] = jnp.zeros((NC, 4, 128), jnp.float32)

    a_in = in_a[...]

    def side_y_copy(q):
        return pltpu.make_async_remote_copy(
            y_out, side_y.at[pos], sys_sem.at[q], syr_sem.at[pos], **to(base + q, pt)
        )

    @pl.when(left & (pos > 0))
    def _():
        @pl.when(unheard)
        def _():
            side_b_copy(0).start()

        y_out[...] = mv(maps[2], a_in) + vecs[1]
        for q in range(LEFT - 1):
            @pl.when(pos > q)
            def _():
                side_y_copy(q).start()

    a1 = jnp.where(is_cut, ghost[...], mv(m0, a_in) + v0)
    vh[0, :, 0:4, :] = a_in
    vh[0, :, 4:8, :] = a1
    a_h = vh[0]
    for i in range(8):
        part = flow_v[:, pl.ds(i, 8, stride=8), :] + c_v[i] + mv(p_v[i], a_h)
        for c in range(NC):
            outs[c][pl.ds(i, 8, stride=8), :] = part[c]
    half_b = mv(w1, a1) + ww1

    for e in range(1, LEFT):
        @pl.when(pos < e)
        def _():
            pltpu.make_async_copy(maps.at[1], side_b.at[e], sbr_sem.at[e]).wait()
            pltpu.make_async_copy(y_out, side_y.at[e], syr_sem.at[e]).wait()

    for e in range(LEFT - 1, 1, -1):
        @pl.when(pos < e - 1)
        def _():
            side_y[e - 1] = mv(side_b[e - 1], side_y[e]) + side_y[e - 1]
            side_b[e - 1] = mm(side_b[e - 1], side_b[e])

    @pl.when(jnp.logical_not(is_mid))
    def _():
        b_copy(0, 0).wait_recv()

    for e in range(1, LEFT):
        @pl.when(pos == e - 1)
        def _():
            in_b[...] = mv(side_b[e], in_b[...]) + side_y[e]

    b_in = in_b[...] * jnp.where(st == NS - 1, 0.0, 1.0)
    vh[1, :, 0:4, :] = (mv(b1, b_in) + half_b) * keep
    vh[1, :, 4:8, :] = b_in
    b_h = vh[1]

    def out_copy(c):
        return pltpu.make_async_copy(outs[c], out.at[c], out_sem.at[c])

    for c in range(NC):
        for i in range(8):
            outs[c][pl.ds(i, 8, stride=8), :] = outs[c][pl.ds(i, 8, stride=8), :] + sum(
                q_v[i, c, k] * b_h[k] for k in range(NC)
            )
        out_copy(c).start()

    for c in range(NC):
        out_copy(c).wait()

    @pl.when(((pos > 0) & left & jnp.logical_not(is_sub)) | near)
    def _():
        map_copy(0).wait_send()

    @pl.when(is_sub)
    def _():
        for k in range(2):
            hop_copy(k).wait_send()
            for q in range(1, SUB + 2):
                if (k, q) != (1, SUB):
                    a_copy(k, q).wait_send()

    @pl.when(near)
    def _():
        map_copy(1).wait_send()

    @pl.when(near | is_cut)
    def _():
        map_copy(2).wait_send()
        w_copy(centre, pos).wait_send()

    @pl.when(jnp.logical_not(is_mid | is_sub))
    def _():
        v_copy().wait_send()

    for q in range(LEFT - 1):
        @pl.when(left & (pos > q))
        def _():
            side_b_copy(q).wait_send()
            side_y_copy(q).wait_send()

    @pl.when(is_mid)
    def _():
        for k, q in a_sent:
            if LEFT <= q < CUT:
                a_copy(k, q).wait_send()


        @pl.when(base == 0)
        def _():
            for k in range(2):
                a_copy(k, CUT).wait_send()

        for k, q in b_sent:
            b_copy(k, q).wait_send()


def to_tiles(x):
    lead = x.shape[:-2]
    x = x.reshape(lead + (2, 8, 4, 128))
    n = len(lead)
    x = jnp.transpose(x, tuple(range(n)) + (n, n + 2, n + 1, n + 3))
    return x.reshape(lead + (64, 128))


def from_tiles(x):
    lead = x.shape[:-2]
    x = x.reshape(lead + (2, 4, 8, 128))
    n = len(lead)
    x = jnp.transpose(x, tuple(range(n)) + (n, n + 2, n + 1, n + 3))
    return x.reshape(lead + (16, 512))


def local(flow_state, residual, spread, diag_inv, lower_jac, upper_jac, partner):
    f32 = jnp.float32
    vm = lambda *s: pltpu.VMEM(s, f32)
    dma = lambda *n: pltpu.SemaphoreType.DMA(n)
    hbm = pl.BlockSpec(memory_space=pltpu.HBM)
    updated = pl.pallas_call(
        kernel,
        out_shape=jax.ShapeDtypeStruct((NC, 64, 128), f32),
        in_specs=[hbm] * 7,
        out_specs=hbm,
        scratch_shapes=[
            vm(64, 128), vm(64, 128), vm(64, 128), vm(64, 128), vm(64, 128), dma(NC),
            vm(5, 64, 128), vm(5, 64, 128), vm(64, 128), vm(25, 64, 128), vm(25, 64, 128), vm(25, 64, 128), vm(5, 64, 128),
            vm(8, 5, 5, 8, 128), vm(8, 5, 5, 8, 128), vm(8, 5, 5, 8, 128), vm(8, 5, 5, 8, 128), vm(8, 5, 5, 8, 128), vm(8, 5, 8, 128),
            vm(5, 2, 8, 128), vm(5, 2, 8, 128), vm(ROW, 5, 4, 128), vm(5, 4, 128), vm(3, 5, 4, 128), vm(4, 5, 4, 128), vm(5, 4, 128),
            vm(3, 5, 5, 4, 128), vm(2, 5, 4, 128), vm(2, 5, 8, 128),
            vm(2, CUT, 3, 5, 5, 4, 128), vm(2, CUT, 2, 5, 4, 128), vm(2, 2, CUT + 1, 5, 4, 128),
            vm(5, 4, 128), vm(5, 4, 128), vm(LEFT, 5, 5, 4, 128), vm(LEFT, 5, 4, 128), vm(5, 4, 128), vm(2, 5, 4, 128),
            pltpu.SMEM((128,), jnp.int32), dma(7), dma(4), dma(4), dma(ROW), dma(ROW), dma(3), dma(3), pltpu.SemaphoreType.REGULAR, pltpu.SemaphoreType.REGULAR,
            dma(3), dma(2, CUT, 3), dma(2), dma(2, CUT, 2), dma(LEFT), dma(LEFT), dma(LEFT), dma(LEFT),
            dma(2, CUT + 1), dma(1), dma(2, CUT + 1), dma(1), dma(2), dma(2),
        ],
        compiler_params=pltpu.CompilerParams(
            collective_id=0, has_side_effects=True, vmem_limit_bytes=60 * 1024 * 1024
        ),
        name="lusgs",
    )(
        to_tiles(flow_state), to_tiles(residual), to_tiles(spread), to_tiles(diag_inv),
        to_tiles(lower_jac), to_tiles(upper_jac), partner,
    )
    return from_tiles(updated)


def solution(mesh):
    blocks = P(None, "stream", "pitch")
    in_specs = (blocks, blocks, P("stream", "pitch"), blocks, blocks, blocks, P())
    return jax.shard_map(local, mesh=mesh, in_specs=in_specs, out_specs=blocks, check_vma=False)
```

```python
import jax
import jax.numpy as jnp
from jax import lax
from jax.experimental import pallas as pl
from jax.experimental.pallas import tpu as pltpu
from jax.sharding import PartitionSpec as P

MESH = pl.DeviceIdType.MESH
NC = 5
NS = 16
NPI = 32
CUT = 8
ROW = 8
MID = 6
LEFT = 5
SUB = 3


def mm(a, b):
    return jnp.stack([sum(a[r, k][None] * b[k] for k in range(NC)) for r in range(NC)])


def mv(a, x):
    return sum(a[:, k] * x[k][None] for k in range(NC))


def kernel(
    flow, res, spr, dinv, low, upp, partner, out,
    out_0, out_1, out_2, out_3, out_4, out_sem, flow_v, res_v, spr_v, d_v, l_v, u_v, src_v,
    s_v, t_v, f_v, q_v, p_v, c_v,
    halo_lo, halo_hi, rot, rots, chosen, facing, ghost,
    maps, vecs, vh, c_maps, c_vecs, answer, in_a, in_b, side_b, side_y, y_out, hop_in,
    part_s, ld_sem, hs_sem, hr_sem, gs_sem, gr_sem, xs_sem, xr_sem, ready, here,
    ms_sem, cm_sem, vs_sem, cv_sem, sbs_sem, sbr_sem, sys_sem, syr_sem, as_sem, ar_sem, bs_sem, br_sem, hs2_sem, hr2_sem,
):
    outs = (out_0, out_1, out_2, out_3, out_4)
    st = lax.axis_index("stream")
    pt = lax.axis_index("pitch")
    up_p, dn_p = lax.rem(pt + 1, NPI), lax.rem(pt + NPI - 1, NPI)
    is_cut = st == CUT
    pos = lax.rem(st, CUT)
    base = st - pos
    core = lax.rem(pt, 2)
    pair = pt - core
    mid = jnp.where(base == 0, MID, MID - 1)
    centre = base + mid
    before = lax.rem(st + NS - CUT + MID, NS)
    is_mid = (pos == mid) & (core == 1)

    def unless_mid(k, q, act):
        if k == 0 or q not in (MID - 1, MID):
            act()
        else:
            pl.when(mid != q)(act)

    left = pos < LEFT
    chained = pos <= SUB
    is_sub = (pos == SUB) & (core == 1)
    home = jnp.where(chained, base + SUB, centre)
    unheard = (base == 0) & (pt == 0)
    near = (pos >= LEFT) & jnp.logical_not(is_mid)
    row = pt // ROW
    row_peers = [row * ROW + lax.rem(pt + d, ROW) for d in range(1, ROW)]
    column_peers = [lax.rem(pt + d * ROW, NPI) for d in range(1, NPI // ROW)]

    def to(stream, pitch):
        return dict(device_id=(stream, pitch), device_id_type=MESH)

    loads = [
        pltpu.make_async_copy(h, v, ld_sem.at[i])
        for i, (h, v) in enumerate(
            ((flow, flow_v), (dinv, d_v), (low, l_v), (upp, u_v), (res, res_v), (spr, spr_v))
        )
    ]

    loads[0].start()
    barrier = pltpu.get_barrier_semaphore()
    for nb in (up_p, dn_p):
        pl.semaphore_signal(barrier, inc=1, **to(st, nb))

    @pl.when(left)
    def _():
        @pl.when(pos >= SUB)
        def _():
            pl.semaphore_signal(barrier, inc=1, **to(centre, pair + 1))

        for q in range(1, LEFT):
            @pl.when((pos < q) & jnp.logical_not(unheard & (pos == 0)))
            def _():
                pl.semaphore_signal(barrier, inc=1, **to(base + q, pt))

    @pl.when(pos == LEFT - 1)
    def _():
        pl.semaphore_signal(barrier, inc=1, **to(base + SUB, pair + 1))

    @pl.when(is_sub)
    def _():
        for q in range(SUB + 1):
            for k in range(2):
                if (k, q) != (1, SUB):
                    pl.semaphore_signal(barrier, inc=1, **to(base + q, pair + k))

    @pl.when(is_mid)
    def _():
        for q in range(LEFT, CUT):
            for k in range(2):
                def greet(q=q, k=k):
                    pl.semaphore_signal(barrier, inc=1, **to(base + q, pair + k))

                unless_mid(k, q, greet)

        @pl.when(base == 0)
        def _():
            for k in range(2):
                pl.semaphore_signal(barrier, inc=1, **to(CUT, pair + k))

    @pl.when(is_cut)
    def _():
        for nb in row_peers + column_peers:
            @pl.when(nb > pt)
            def _():
                pl.semaphore_signal(barrier, inc=1, **to(st, nb))

    for c in loads[1:]:
        c.start()

    expected = (
        2 + jnp.where(is_cut, pt - row * ROW + row + 1, 0) + jnp.where(is_mid, 2 * (LEFT - SUB), 0)
        + jnp.where(near | (chained & jnp.logical_not(is_sub)), 1, 0) + jnp.where(is_sub, 2, 0)
        + jnp.where(left & (pos > 0), pos - jnp.where(unheard, 1, 0), 0)
    )
    pl.semaphore_wait(barrier, expected)

    @pl.when(is_mid)
    def _():
        for q, k in ((LEFT - 1, 0), (LEFT - 1, 1), (SUB, 1)):
            pl.semaphore_signal(ready, inc=1, **to(base + q, pair + k))

    @pl.when(is_cut)
    def _():
        for nb in row_peers + column_peers:
            @pl.when(nb < pt)
            def _():
                pl.semaphore_signal(here, inc=1, **to(st, nb))

    loads[0].wait()

    def halos():
        copies = []
        for h in range(2):
            copies.append(
                pltpu.make_async_remote_copy(
                    flow_v.at[:, pl.ds(h * 32 + 24, 8), :], halo_lo.at[:, h],
                    hs_sem.at[h], hr_sem.at[h], **to(st, up_p),
                )
            )
            copies.append(
                pltpu.make_async_remote_copy(
                    flow_v.at[:, pl.ds(h * 32, 8), :], halo_hi.at[:, h],
                    hs_sem.at[2 + h], hr_sem.at[2 + h], **to(st, dn_p),
                )
            )
        return copies

    for c in halos():
        c.start()

    def row_copies():
        return [
            pltpu.make_async_remote_copy(
                rots, rot.at[lax.rem(pt, ROW)], gs_sem.at[d], gr_sem.at[d], **to(st, nb)
            )
            for d, nb in enumerate(row_peers)
        ]

    def column_copies():
        return [
            pltpu.make_async_remote_copy(
                chosen.at[d], facing.at[row], xs_sem.at[d], xr_sem.at[d], **to(st, nb)
            )
            for d, nb in enumerate(column_peers)
        ]

    def choose(target, nb):
        for k in range(4):
            who = part_s[nb * 4 + k]
            target[:, k : k + 1, :] = rot[lax.rem(who // 4, ROW), :, pl.ds(lax.rem(who, 4), 1), :]

    for c in loads[1:4]:
        c.wait()

    def block(ref, i):
        return ref[:, pl.ds(i, 8, stride=8), :].reshape(NC, NC, 8, 128)

    def first(i, f):
        s = mm(block(d_v, i), block(l_v, i))
        s_v[i] = s
        f = jnp.where(i == 0, s, mm(s, f))
        f_v[i] = f
        return f

    lax.fori_loop(0, 8, lambda i, _: (first(i, f_v[jnp.maximum(i - 1, 0)]), 0)[1], 0)

    keep = jnp.where(is_cut, 0.0, 1.0)
    m0, m1 = f_v[7, :, :, 0:4, :], f_v[7, :, :, 4:8, :]
    maps[0] = mm(m1, m0)

    @pl.when(is_cut)
    def _():
        rots[...] = flow_v[:, pl.ds(7, 4, stride=8), :]
        rot[lax.rem(pt, ROW)] = flow_v[:, pl.ds(7, 4, stride=8), :]
        pltpu.make_async_copy(partner, part_s, ld_sem.at[6]).start()
        higher = len(row_peers) + len(column_peers) - (pt - row * ROW) - row

        @pl.when(higher > 0)
        def _():
            pl.semaphore_wait(here, higher)

        for c in row_copies():
            c.start()

    def map_copy(k, stream=home):
        slot = pos
        return pltpu.make_async_remote_copy(
            maps.at[k], c_maps.at[core, slot, k], ms_sem.at[k], cm_sem.at[core, slot, k], **to(stream, pair + 1)
        )

    @pl.when(near | (chained & jnp.logical_not(is_sub) & (pos > 0)))
    def _():
        map_copy(0).start()

    def last(j, _):
        i = 7 - j
        n = jnp.minimum(i + 1, 7)
        t = mm(block(d_v, i), block(u_v, i))
        t_v[i] = t
        q_v[i] = jnp.where(i == 7, t, mm(t, q_v[n]))
        p_v[i] = f_v[i] + jnp.where(i == 7, 0.0, mm(t, p_v[n]))
        return 0

    lax.fori_loop(0, 8, last, 0)

    b0, b1 = q_v[0, :, :, 0:4, :], q_v[0, :, :, 4:8, :]
    maps[1] = mm(b0, b1)
    w0, w1 = p_v[0, :, :, 0:4, :], p_v[0, :, :, 4:8, :]
    maps[2] = w0 + mm(b0, mm(w1, m0)) * keep

    def side_b_copy(q):
        return pltpu.make_async_remote_copy(
            maps.at[1], side_b.at[pos], sbs_sem.at[q], sbr_sem.at[pos], **to(base + q, pt)
        )

    @pl.when(near)
    def _():
        map_copy(1).start()
        map_copy(2).start()

    @pl.when(is_cut)
    def _():
        map_copy(2, before).start()

    for q in range(LEFT - 1):
        @pl.when(left & (pos > q) & ((q > 0) | jnp.logical_not(unheard)))
        def _():
            side_b_copy(q).start()

    for c in loads[4:]:
        c.wait()
    for c in halos():
        c.wait()

    for h in range(2):
        for c in range(4):
            r = h * 32 + c * 8
            here_v = flow_v[:, r : r + 8, :]
            lo = halo_lo[:, h] if c == 0 else flow_v[:, r - 8 : r, :]
            hi = halo_hi[:, h] if c == 3 else flow_v[:, r + 8 : r + 16, :]
            src_v[:, r : r + 8, :] = res_v[:, r : r + 8, :] + spr_v[r : r + 8, :][None] * (
                hi + lo - 2.0 * here_v
            )

    star = None
    for i in range(8):
        now = mv(block(d_v, i), src_v[:, pl.ds(i, 8, stride=8), :])
        star = now if star is None else now + mv(s_v[i], star)
        c_v[i] = star
    vh[0] = star
    v0, v1 = vh[0, :, 0:4, :], vh[0, :, 4:8, :]
    ghost[...] = v0

    def v_copy():
        return pltpu.make_async_remote_copy(
            vecs.at[0], c_vecs.at[core, pos, 0], vs_sem.at[0], cv_sem.at[core, pos, 0], **to(home, pair + 1)
        )

    def w_copy(stream, slot):
        return pltpu.make_async_remote_copy(
            vecs.at[1], c_vecs.at[core, slot, 1], vs_sem.at[1], cv_sem.at[core, slot, 1], **to(stream, pair + 1)
        )

    @pl.when(jnp.logical_not(is_cut))
    def _():
        vecs[0] = mv(m1, v0) + v1

        @pl.when(near)
        def _():
            v_copy().start()

    ch = star
    for i in range(6, -1, -1):
        ch = c_v[i] + mv(t_v[i], ch)
        c_v[i] = ch
    vh[1] = ch
    ww0, ww1 = vh[1, :, 0:4, :], vh[1, :, 4:8, :]
    vecs[1] = ww0 + mv(b0, mv(w1, v0) + ww1) * keep

    @pl.when(near)
    def _():
        w_copy(centre, pos).start()

    @pl.when(is_cut)
    def _():
        w_copy(before, 0).start()

    @pl.when(left & jnp.logical_not(is_cut) & jnp.logical_not(is_sub))
    def _():
        @pl.when(jnp.logical_not(chained))
        def _():
            pl.semaphore_wait(ready, 1)

        v_copy().start()

        @pl.when((pos > 0) & jnp.logical_not(chained))
        def _():
            map_copy(0).start()

    @pl.when(is_cut)
    def _():
        pltpu.make_async_copy(partner, part_s, ld_sem.at[6]).wait()
        for c in row_copies():
            c.wait()
        choose(facing.at[row], pt)
        for d, c in enumerate(column_copies()):
            choose(chosen.at[d], column_peers[d])
            c.start()

    @pl.when(is_cut)
    def _():
        for c in column_copies():
            c.wait()
        for k in range(4):
            who = part_s[pt * 4 + k]
            ghost[:, k : k + 1, :] = facing[who // (4 * ROW), :, pl.ds(k, 1), :]
        vecs[0] = mv(m1, ghost[...]) + v1
        v_copy().start()

    def a_copy(k, q):
        return pltpu.make_async_remote_copy(
            answer.at[0, k, q], in_a, as_sem.at[k, q], ar_sem.at[0], **to(lax.rem(base + q, NS), pair + k)
        )

    def b_copy(k, q):
        return pltpu.make_async_remote_copy(
            answer.at[1, k, max(q, LEFT - 1)], in_b, bs_sem.at[k, q], br_sem.at[0], **to(base + q, pair + k)
        )

    def arrived_map(k, q, m):
        pltpu.make_async_copy(maps.at[m], c_maps.at[k, q, m], cm_sem.at[k, q, m]).wait()

    def arrived_vec(k, q, m):
        pltpu.make_async_copy(vecs.at[m], c_vecs.at[k, q, m], cv_sem.at[k, q, m]).wait()

    def hop_copy(k):
        return pltpu.make_async_remote_copy(
            answer.at[0, k, SUB + 1], hop_in.at[k], hs2_sem.at[k], hr2_sem.at[k], **to(centre, pt)
        )

    a_sent = [(k, q) for q in range(1, CUT + 1) for k in range(2)]
    b_sent = [(k, q) for q in range(CUT) for k in range(2)]

    @pl.when(is_sub)
    def _():
        c_maps[1, SUB, 0] = maps[0]
        c_vecs[1, SUB, 0] = vecs[0]
        def early(k):
            for q in range(SUB + 1):
                if (k, q) != (1, SUB):
                    if q:
                        arrived_map(k, q, 0)
                    arrived_vec(k, q, 0)
            hop = c_vecs[k, 0, 0]
            for q in range(1, SUB + 2):
                answer[0, k, q] = hop
                if q <= SUB:
                    hop = mv(c_maps[k, q, 0], hop) + c_vecs[k, q, 0]

        def tell(k):
            hop_copy(k).start()
            for q in range(SUB + 1, 0, -1):
                if (k, q) != (1, SUB):
                    a_copy(k, q).start()
            if k == 1:
                in_a[...] = answer[0, 1, SUB]

        @pl.when(base == 0)
        def _():
            early(1)
            for q in range(SUB + 1, 0, -1):
                if q != SUB:
                    a_copy(1, q).start()
            in_a[...] = answer[0, 1, SUB]
            pl.semaphore_wait(ready, 1)
            hop_copy(1).start()
            early(0)
            tell(0)

        @pl.when(base != 0)
        def _():
            pl.semaphore_wait(ready, 1)
            early(0)
            early(1)
            tell(0)
            tell(1)

    def arrived_right(k):
        arrived_map(k, LEFT - 1, 0)
        arrived_vec(k, LEFT - 1, 0)
        for q in range(LEFT, CUT):
            def arrived(q=q):
                for m in range(3):
                    arrived_map(k, q, m)
                for m in range(2):
                    arrived_vec(k, q, m)

            unless_mid(k, q, arrived)
        for q in range(CUT - 2, LEFT - 1, -1):
            c_maps[k, q - LEFT, 1] = mm(c_maps[k, q, 1], c_maps[k, q + 1, 1] if q == CUT - 2 else c_maps[k, q + 1 - LEFT, 1])

        @pl.when(base == 0)
        def _():
            arrived_map(k, 0, 2)

        @pl.when(base != 0)
        def _():
            c_maps[k, 0, 2] = jnp.zeros((NC, NC, 4, 128), jnp.float32)
            c_vecs[k, 0, 1] = jnp.zeros((NC, 4, 128), jnp.float32)

    def right_values(k, a, stop):
        for q in range(LEFT, CUT):
            answer[0, k, q] = a
            a = mv(c_maps[k, q, 0], a) + c_vecs[k, q, 0]
        answer[0, k, CUT] = a
        b = mv(c_maps[k, 0, 2], a)
        answer[1, k, CUT - 1] = b
        for q in range(CUT - 1, stop, -1):
            b = mv(c_maps[k, q, 1], b) + mv(c_maps[k, q, 2], answer[0, k, q]) + c_vecs[k, q, 1]
            answer[1, k, q - 1] = b

    def heard(k):
        hop_copy(k).wait_recv()
        answer[0, k, LEFT - 1] = hop_in[k]
        return mv(c_maps[k, LEFT - 1, 0], hop_in[k]) + c_vecs[k, LEFT - 1, 0]

    def solve(k):
        arrived_right(k)
        a = heard(k)
        right_values(k, a, LEFT - 1)

    def prepare(k):
        arrived_right(k)
        back = c_maps[k, 0, 2]
        for q in range(CUT - 1, LEFT - 1, -1):
            back = c_maps[k, q, 2] + mm(c_maps[k, q, 1], mm(back, c_maps[k, q, 0]))
        c_maps[k, LEFT - 2, 1] = mm(back, c_maps[k, LEFT - 1, 0])
        right_values(k, c_vecs[k, LEFT - 1, 0], LEFT - 1)

    def finish(k, late):
        if late:
            hop_copy(k).wait_recv()
            answer[1, k, LEFT - 1] = answer[1, k, LEFT - 1] + mv(c_maps[k, LEFT - 2, 1], hop_in[k])

        @pl.when(base == 0)
        def _():
            arrived_vec(k, 0, 1)

        w = c_vecs[k, 0, 1]
        answer[1, k, LEFT - 1] = answer[1, k, LEFT - 1] + mv(c_maps[k, 0, 1], w)
        b_copy(k, 0).start()

    def finish_left(cores):
        for j in range(1, LEFT):
            for k in cores:
                b_copy(k, j).start()

    def finish_right(k, late):
        if late:
            right_values(k, mv(c_maps[k, LEFT - 1, 0], hop_in[k]) + c_vecs[k, LEFT - 1, 0], LEFT)
        w = c_vecs[k, 0, 1]
        for q in range(LEFT, CUT):
            if q == CUT - 1:
                more = w
            else:
                more = mv(c_maps[k, CUT - 1, 1] if q == CUT - 2 else c_maps[k, q + 1 - LEFT, 1], w)
            answer[1, k, q] = answer[1, k, q] + more

            def answers(q=q):
                b_copy(k, q).start()
                a_copy(k, q).start()

            unless_mid(k, q, answers)

        @pl.when(base == 0)
        def _():
            a_copy(k, CUT).start()

        if k == 1:
            in_a[...] = answer[0, 1, mid]
            in_b[...] = answer[1, 1, mid]

    @pl.when(is_mid)
    def _():
        c_maps[1, mid] = maps[...]
        c_vecs[1, mid] = vecs[...]

        @pl.when(base != 0)
        def _():
            prepare(1)
            prepare(0)
            finish(0, True)
            finish(1, True)
            finish_left((0, 1))
            finish_right(0, True)
            finish_right(1, True)

        @pl.when((base == 0) & (pair == 0))
        def _():
            solve(1)
            finish(1, False)
            finish_left((1,))
            prepare(0)
            finish(0, True)
            finish_left((0,))
            finish_right(1, False)
            finish_right(0, True)

        @pl.when((base == 0) & (pair != 0))
        def _():
            solve(1)
            solve(0)
            finish(0, False)
            finish(1, False)
            finish_left((0, 1))
            finish_right(0, False)
            finish_right(1, False)

    @pl.when(jnp.logical_not(is_mid | is_sub) & (st != 0))
    def _():
        a_copy(0, 1).wait_recv()

    @pl.when(st == 0)
    def _():
        in_a[...] = jnp.zeros((NC, 4, 128), jnp.float32)

    a_in = in_a[...]

    def side_y_copy(q):
        return pltpu.make_async_remote_copy(
            y_out, side_y.at[pos], sys_sem.at[q], syr_sem.at[pos], **to(base + q, pt)
        )

    @pl.when(left & (pos > 0))
    def _():
        @pl.when(unheard)
        def _():
            side_b_copy(0).start()

        y_out[...] = mv(maps[2], a_in) + vecs[1]
        for q in range(LEFT - 1):
            @pl.when(pos > q)
            def _():
                side_y_copy(q).start()

    a1 = jnp.where(is_cut, ghost[...], mv(m0, a_in) + v0)
    vh[0, :, 0:4, :] = a_in
    vh[0, :, 4:8, :] = a1
    a_h = vh[0]
    for i in range(8):
        part = flow_v[:, pl.ds(i, 8, stride=8), :] + c_v[i] + mv(p_v[i], a_h)
        for c in range(NC):
            outs[c][pl.ds(i, 8, stride=8), :] = part[c]
    half_b = mv(w1, a1) + ww1

    for e in range(1, LEFT):
        @pl.when(pos < e)
        def _():
            pltpu.make_async_copy(maps.at[1], side_b.at[e], sbr_sem.at[e]).wait()
            pltpu.make_async_copy(y_out, side_y.at[e], syr_sem.at[e]).wait()

    for e in range(LEFT - 1, 1, -1):
        @pl.when(pos < e - 1)
        def _():
            side_y[e - 1] = mv(side_b[e - 1], side_y[e]) + side_y[e - 1]
            side_b[e - 1] = mm(side_b[e - 1], side_b[e])

    @pl.when(jnp.logical_not(is_mid))
    def _():
        b_copy(0, 0).wait_recv()

    for e in range(1, LEFT):
        @pl.when(pos == e - 1)
        def _():
            in_b[...] = mv(side_b[e], in_b[...]) + side_y[e]

    b_in = in_b[...] * jnp.where(st == NS - 1, 0.0, 1.0)
    vh[1, :, 0:4, :] = (mv(b1, b_in) + half_b) * keep
    vh[1, :, 4:8, :] = b_in
    b_h = vh[1]

    def out_copy(c):
        return pltpu.make_async_copy(outs[c], out.at[c], out_sem.at[c])

    for c in range(NC):
        for i in range(8):
            outs[c][pl.ds(i, 8, stride=8), :] = outs[c][pl.ds(i, 8, stride=8), :] + sum(
                q_v[i, c, k] * b_h[k] for k in range(NC)
            )
        out_copy(c).start()

    for c in range(NC):
        out_copy(c).wait()

    @pl.when(((pos > 0) & left & jnp.logical_not(is_sub)) | near)
    def _():
        map_copy(0).wait_send()

    @pl.when(is_sub)
    def _():
        for k in range(2):
            hop_copy(k).wait_send()
            for q in range(1, SUB + 2):
                if (k, q) != (1, SUB):
                    a_copy(k, q).wait_send()

    @pl.when(near)
    def _():
        map_copy(1).wait_send()

    @pl.when(near | is_cut)
    def _():
        map_copy(2).wait_send()
        w_copy(centre, pos).wait_send()

    @pl.when(jnp.logical_not(is_mid | is_sub))
    def _():
        v_copy().wait_send()

    for q in range(LEFT - 1):
        @pl.when(left & (pos > q))
        def _():
            side_b_copy(q).wait_send()
            side_y_copy(q).wait_send()

    @pl.when(is_mid)
    def _():
        for k, q in a_sent:
            if LEFT <= q < CUT:
                unless_mid(k, q, lambda k=k, q=q: a_copy(k, q).wait_send())


        @pl.when(base == 0)
        def _():
            for k in range(2):
                a_copy(k, CUT).wait_send()

        for k, q in b_sent:
            unless_mid(k, q, lambda k=k, q=q: b_copy(k, q).wait_send())


def to_tiles(x):
    lead = x.shape[:-2]
    x = x.reshape(lead + (2, 8, 4, 128))
    n = len(lead)
    x = jnp.transpose(x, tuple(range(n)) + (n, n + 2, n + 1, n + 3))
    return x.reshape(lead + (64, 128))


def from_tiles(x):
    lead = x.shape[:-2]
    x = x.reshape(lead + (2, 4, 8, 128))
    n = len(lead)
    x = jnp.transpose(x, tuple(range(n)) + (n, n + 2, n + 1, n + 3))
    return x.reshape(lead + (16, 512))


def local(flow_state, residual, spread, diag_inv, lower_jac, upper_jac, partner):
    f32 = jnp.float32
    vm = lambda *s: pltpu.VMEM(s, f32)
    dma = lambda *n: pltpu.SemaphoreType.DMA(n)
    hbm = pl.BlockSpec(memory_space=pltpu.HBM)
    updated = pl.pallas_call(
        kernel,
        out_shape=jax.ShapeDtypeStruct((NC, 64, 128), f32),
        in_specs=[hbm] * 7,
        out_specs=hbm,
        scratch_shapes=[
            vm(64, 128), vm(64, 128), vm(64, 128), vm(64, 128), vm(64, 128), dma(NC),
            vm(5, 64, 128), vm(5, 64, 128), vm(64, 128), vm(25, 64, 128), vm(25, 64, 128), vm(25, 64, 128), vm(5, 64, 128),
            vm(8, 5, 5, 8, 128), vm(8, 5, 5, 8, 128), vm(8, 5, 5, 8, 128), vm(8, 5, 5, 8, 128), vm(8, 5, 5, 8, 128), vm(8, 5, 8, 128),
            vm(5, 2, 8, 128), vm(5, 2, 8, 128), vm(ROW, 5, 4, 128), vm(5, 4, 128), vm(3, 5, 4, 128), vm(4, 5, 4, 128), vm(5, 4, 128),
            vm(3, 5, 5, 4, 128), vm(2, 5, 4, 128), vm(2, 5, 8, 128),
            vm(2, CUT, 3, 5, 5, 4, 128), vm(2, CUT, 2, 5, 4, 128), vm(2, 2, CUT + 1, 5, 4, 128),
            vm(5, 4, 128), vm(5, 4, 128), vm(LEFT, 5, 5, 4, 128), vm(LEFT, 5, 4, 128), vm(5, 4, 128), vm(2, 5, 4, 128),
            pltpu.SMEM((128,), jnp.int32), dma(7), dma(4), dma(4), dma(ROW), dma(ROW), dma(3), dma(3), pltpu.SemaphoreType.REGULAR, pltpu.SemaphoreType.REGULAR,
            dma(3), dma(2, CUT, 3), dma(2), dma(2, CUT, 2), dma(LEFT), dma(LEFT), dma(LEFT), dma(LEFT),
            dma(2, CUT + 1), dma(1), dma(2, CUT + 1), dma(1), dma(2), dma(2),
        ],
        compiler_params=pltpu.CompilerParams(
            collective_id=0, has_side_effects=True, vmem_limit_bytes=60 * 1024 * 1024
        ),
        name="lusgs",
    )(
        to_tiles(flow_state), to_tiles(residual), to_tiles(spread), to_tiles(diag_inv),
        to_tiles(lower_jac), to_tiles(upper_jac), partner,
    )
    return from_tiles(updated)


def solution(mesh):
    blocks = P(None, "stream", "pitch")
    in_specs = (blocks, blocks, P("stream", "pitch"), blocks, blocks, blocks, P())
    return jax.shard_map(local, mesh=mesh, in_specs=in_specs, out_specs=blocks, check_vma=False)
```

```python
import jax
import jax.numpy as jnp
from jax import lax
from jax.experimental import pallas as pl
from jax.experimental.pallas import tpu as pltpu
from jax.sharding import PartitionSpec as P

MESH = pl.DeviceIdType.MESH
NC = 5
NS = 16
NPI = 32
CUT = 8
ROW = 8
MID = 6
LEFT = 5
SUB = 3


def mm(a, b):
    return jnp.stack([sum(a[r, k][None] * b[k] for k in range(NC)) for r in range(NC)])


def mv(a, x):
    return sum(a[:, k] * x[k][None] for k in range(NC))


def kernel(
    flow, res, spr, dinv, low, upp, partner, out,
    out_0, out_1, out_2, out_3, out_4, out_sem, flow_v, res_v, spr_v, d_v, l_v, u_v, src_v,
    s_v, t_v, f_v, q_v, p_v, c_v,
    halo_lo, halo_hi, rot, rots, chosen, facing, ghost,
    maps, vecs, vh, c_maps, c_vecs, answer, in_a, in_b, side_b, side_y, y_out, hop_in,
    part_s, ld_sem, hs_sem, hr_sem, gs_sem, gr_sem, xs_sem, xr_sem, ready, here,
    ms_sem, cm_sem, vs_sem, cv_sem, sbs_sem, sbr_sem, sys_sem, syr_sem, as_sem, ar_sem, bs_sem, br_sem, hs2_sem, hr2_sem,
):
    outs = (out_0, out_1, out_2, out_3, out_4)
    st = lax.axis_index("stream")
    pt = lax.axis_index("pitch")
    up_p, dn_p = lax.rem(pt + 1, NPI), lax.rem(pt + NPI - 1, NPI)
    is_cut = st == CUT
    pos = lax.rem(st, CUT)
    base = st - pos
    core = lax.rem(pt, 2)
    pair = pt - core
    mid = jnp.where(base == 0, MID, MID - 1)
    centre = base + mid
    before = lax.rem(st + NS - CUT + MID, NS)
    is_mid = (pos == mid) & (core == 1)

    def unless_mid(k, q, act):
        if k == 0 or q not in (MID - 1, MID):
            act()
        else:
            pl.when(mid != q)(act)

    left = pos < LEFT
    chained = pos <= SUB
    is_sub = (pos == SUB) & (core == 1)
    home = jnp.where(chained, base + SUB, centre)
    unheard = (base == 0) & (pt == 0)
    near = (pos >= LEFT) & jnp.logical_not(is_mid)
    row = pt // ROW
    row_peers = [row * ROW + lax.rem(pt + d, ROW) for d in range(1, ROW)]
    column_peers = [lax.rem(pt + d * ROW, NPI) for d in range(1, NPI // ROW)]

    def to(stream, pitch):
        return dict(device_id=(stream, pitch), device_id_type=MESH)

    loads = [
        pltpu.make_async_copy(h, v, ld_sem.at[i])
        for i, (h, v) in enumerate(
            ((flow, flow_v), (dinv, d_v), (low, l_v), (upp, u_v), (res, res_v), (spr, spr_v))
        )
    ]

    loads[0].start()
    barrier = pltpu.get_barrier_semaphore()
    for nb in (up_p, dn_p):
        pl.semaphore_signal(barrier, inc=1, **to(st, nb))

    @pl.when(left)
    def _():
        @pl.when(pos >= SUB)
        def _():
            pl.semaphore_signal(barrier, inc=1, **to(centre, pair + 1))

        for q in range(1, LEFT):
            @pl.when((pos < q) & jnp.logical_not(unheard & (pos == 0)))
            def _():
                pl.semaphore_signal(barrier, inc=1, **to(base + q, pt))

    @pl.when(pos == LEFT - 1)
    def _():
        pl.semaphore_signal(barrier, inc=1, **to(base + SUB, pair + 1))

    @pl.when(is_sub)
    def _():
        for q in range(SUB + 1):
            for k in range(2):
                if (k, q) != (1, SUB):
                    pl.semaphore_signal(barrier, inc=1, **to(base + q, pair + k))

    @pl.when(is_mid)
    def _():
        for q in range(LEFT, CUT):
            for k in range(2):
                def greet(q=q, k=k):
                    pl.semaphore_signal(barrier, inc=1, **to(base + q, pair + k))

                unless_mid(k, q, greet)

        @pl.when(base == 0)
        def _():
            for k in range(2):
                pl.semaphore_signal(barrier, inc=1, **to(CUT, pair + k))

    @pl.when(is_cut)
    def _():
        for nb in row_peers + column_peers:
            @pl.when(nb > pt)
            def _():
                pl.semaphore_signal(barrier, inc=1, **to(st, nb))

    for c in loads[1:]:
        c.start()

    expected = (
        2 + jnp.where(is_cut, pt - row * ROW + row + 1, 0) + jnp.where(is_mid, 2 * (LEFT - SUB), 0)
        + jnp.where(near | (chained & jnp.logical_not(is_sub)), 1, 0) + jnp.where(is_sub, 2, 0)
        + jnp.where(left & (pos > 0), pos - jnp.where(unheard, 1, 0), 0)
    )
    pl.semaphore_wait(barrier, expected)

    @pl.when(is_mid)
    def _():
        for q, k in ((LEFT - 1, 0), (LEFT - 1, 1), (SUB, 1)):
            pl.semaphore_signal(ready, inc=1, **to(base + q, pair + k))

    @pl.when(is_cut)
    def _():
        for nb in row_peers + column_peers:
            @pl.when(nb < pt)
            def _():
                pl.semaphore_signal(here, inc=1, **to(st, nb))

    loads[0].wait()

    def halos():
        copies = []
        for h in range(2):
            copies.append(
                pltpu.make_async_remote_copy(
                    flow_v.at[:, pl.ds(h * 32 + 24, 8), :], halo_lo.at[:, h],
                    hs_sem.at[h], hr_sem.at[h], **to(st, up_p),
                )
            )
            copies.append(
                pltpu.make_async_remote_copy(
                    flow_v.at[:, pl.ds(h * 32, 8), :], halo_hi.at[:, h],
                    hs_sem.at[2 + h], hr_sem.at[2 + h], **to(st, dn_p),
                )
            )
        return copies

    for c in halos():
        c.start()

    def row_copies():
        return [
            pltpu.make_async_remote_copy(
                rots, rot.at[lax.rem(pt, ROW)], gs_sem.at[d], gr_sem.at[d], **to(st, nb)
            )
            for d, nb in enumerate(row_peers)
        ]

    def column_copies():
        return [
            pltpu.make_async_remote_copy(
                chosen.at[d], facing.at[row], xs_sem.at[d], xr_sem.at[d], **to(st, nb)
            )
            for d, nb in enumerate(column_peers)
        ]

    def choose(target, nb):
        for k in range(4):
            who = part_s[nb * 4 + k]
            target[:, k : k + 1, :] = rot[lax.rem(who // 4, ROW), :, pl.ds(lax.rem(who, 4), 1), :]

    for c in loads[1:4]:
        c.wait()

    def block(ref, i):
        return ref[:, pl.ds(i, 8, stride=8), :].reshape(NC, NC, 8, 128)

    def first(i, f):
        s = mm(block(d_v, i), block(l_v, i))
        s_v[i] = s
        f = jnp.where(i == 0, s, mm(s, f))
        f_v[i] = f
        return f

    lax.fori_loop(0, 8, lambda i, _: (first(i, f_v[jnp.maximum(i - 1, 0)]), 0)[1], 0)

    keep = jnp.where(is_cut, 0.0, 1.0)
    m0, m1 = f_v[7, :, :, 0:4, :], f_v[7, :, :, 4:8, :]
    maps[0] = mm(m1, m0)

    @pl.when(is_cut)
    def _():
        rots[...] = flow_v[:, pl.ds(7, 4, stride=8), :]
        rot[lax.rem(pt, ROW)] = flow_v[:, pl.ds(7, 4, stride=8), :]
        pltpu.make_async_copy(partner, part_s, ld_sem.at[6]).start()
        higher = len(row_peers) + len(column_peers) - (pt - row * ROW) - row

        @pl.when(higher > 0)
        def _():
            pl.semaphore_wait(here, higher)

        for c in row_copies():
            c.start()

    def map_copy(k, stream=home):
        slot = pos
        return pltpu.make_async_remote_copy(
            maps.at[k], c_maps.at[core, slot, k], ms_sem.at[k], cm_sem.at[core, slot, k], **to(stream, pair + 1)
        )

    @pl.when(near | (chained & jnp.logical_not(is_sub) & (pos > 0)))
    def _():
        map_copy(0).start()

    def last(j, _):
        i = 7 - j
        n = jnp.minimum(i + 1, 7)
        t = mm(block(d_v, i), block(u_v, i))
        t_v[i] = t
        q_v[i] = jnp.where(i == 7, t, mm(t, q_v[n]))
        p_v[i] = f_v[i] + jnp.where(i == 7, 0.0, mm(t, p_v[n]))
        return 0

    lax.fori_loop(0, 8, last, 0)

    b0, b1 = q_v[0, :, :, 0:4, :], q_v[0, :, :, 4:8, :]
    maps[1] = mm(b0, b1)
    w0, w1 = p_v[0, :, :, 0:4, :], p_v[0, :, :, 4:8, :]
    maps[2] = w0 + mm(b0, mm(w1, m0)) * keep

    def side_b_copy(q):
        return pltpu.make_async_remote_copy(
            maps.at[1], side_b.at[pos], sbs_sem.at[q], sbr_sem.at[pos], **to(base + q, pt)
        )

    @pl.when(near)
    def _():
        map_copy(1).start()
        map_copy(2).start()

    @pl.when(is_cut)
    def _():
        map_copy(2, before).start()

    for q in range(LEFT - 1):
        @pl.when(left & (pos > q) & ((q > 0) | jnp.logical_not(unheard)))
        def _():
            side_b_copy(q).start()

    for c in loads[4:]:
        c.wait()
    for c in halos():
        c.wait()

    for h in range(2):
        for c in range(4):
            r = h * 32 + c * 8
            here_v = flow_v[:, r : r + 8, :]
            lo = halo_lo[:, h] if c == 0 else flow_v[:, r - 8 : r, :]
            hi = halo_hi[:, h] if c == 3 else flow_v[:, r + 8 : r + 16, :]
            src_v[:, r : r + 8, :] = res_v[:, r : r + 8, :] + spr_v[r : r + 8, :][None] * (
                hi + lo - 2.0 * here_v
            )

    star = None
    for i in range(8):
        now = mv(block(d_v, i), src_v[:, pl.ds(i, 8, stride=8), :])
        star = now if star is None else now + mv(s_v[i], star)
        c_v[i] = star
    vh[0] = star
    v0, v1 = vh[0, :, 0:4, :], vh[0, :, 4:8, :]
    ghost[...] = v0

    def v_copy():
        return pltpu.make_async_remote_copy(
            vecs.at[0], c_vecs.at[core, pos, 0], vs_sem.at[0], cv_sem.at[core, pos, 0], **to(home, pair + 1)
        )

    def w_copy(stream, slot):
        return pltpu.make_async_remote_copy(
            vecs.at[1], c_vecs.at[core, slot, 1], vs_sem.at[1], cv_sem.at[core, slot, 1], **to(stream, pair + 1)
        )

    @pl.when(jnp.logical_not(is_cut))
    def _():
        vecs[0] = mv(m1, v0) + v1

        @pl.when(near)
        def _():
            v_copy().start()

    ch = star
    for i in range(6, -1, -1):
        ch = c_v[i] + mv(t_v[i], ch)
        c_v[i] = ch
    vh[1] = ch
    ww0, ww1 = vh[1, :, 0:4, :], vh[1, :, 4:8, :]
    vecs[1] = ww0 + mv(b0, mv(w1, v0) + ww1) * keep

    @pl.when(near)
    def _():
        w_copy(centre, pos).start()

    @pl.when(is_cut)
    def _():
        w_copy(before, 0).start()

    @pl.when(left & jnp.logical_not(is_cut) & jnp.logical_not(is_sub))
    def _():
        @pl.when(jnp.logical_not(chained))
        def _():
            pl.semaphore_wait(ready, 1)

        v_copy().start()

        @pl.when((pos > 0) & jnp.logical_not(chained))
        def _():
            map_copy(0).start()

    @pl.when(is_cut)
    def _():
        pltpu.make_async_copy(partner, part_s, ld_sem.at[6]).wait()
        for c in row_copies():
            c.wait()
        choose(facing.at[row], pt)
        for d, c in enumerate(column_copies()):
            choose(chosen.at[d], column_peers[d])
            c.start()

    @pl.when(is_cut)
    def _():
        for c in column_copies():
            c.wait()
        for k in range(4):
            who = part_s[pt * 4 + k]
            ghost[:, k : k + 1, :] = facing[who // (4 * ROW), :, pl.ds(k, 1), :]
        vecs[0] = mv(m1, ghost[...]) + v1
        v_copy().start()

    def a_copy(k, q):
        return pltpu.make_async_remote_copy(
            answer.at[0, k, q], in_a, as_sem.at[k, q], ar_sem.at[0], **to(lax.rem(base + q, NS), pair + k)
        )

    def b_copy(k, q):
        return pltpu.make_async_remote_copy(
            answer.at[1, k, max(q, LEFT - 1)], in_b, bs_sem.at[k, q], br_sem.at[0], **to(base + q, pair + k)
        )

    def arrived_map(k, q, m):
        pltpu.make_async_copy(maps.at[m], c_maps.at[k, q, m], cm_sem.at[k, q, m]).wait()

    def arrived_vec(k, q, m):
        pltpu.make_async_copy(vecs.at[m], c_vecs.at[k, q, m], cv_sem.at[k, q, m]).wait()

    def hop_copy(k):
        return pltpu.make_async_remote_copy(
            answer.at[0, k, SUB + 1], hop_in.at[k], hs2_sem.at[k], hr2_sem.at[k], **to(centre, pt)
        )

    a_sent = [(k, q) for q in range(1, CUT + 1) for k in range(2)]
    b_sent = [(k, q) for q in range(CUT) for k in range(2)]

    @pl.when(is_sub)
    def _():
        c_maps[1, SUB, 0] = maps[0]
        c_vecs[1, SUB, 0] = vecs[0]
        def early(k):
            for q in range(SUB + 1):
                if (k, q) != (1, SUB):
                    if q:
                        arrived_map(k, q, 0)
                    arrived_vec(k, q, 0)
            hop = c_vecs[k, 0, 0]
            for q in range(1, SUB + 2):
                answer[0, k, q] = hop
                if q <= SUB:
                    hop = mv(c_maps[k, q, 0], hop) + c_vecs[k, q, 0]

        def tell(k):
            hop_copy(k).start()
            for q in range(SUB + 1, 0, -1):
                if (k, q) != (1, SUB):
                    a_copy(k, q).start()
            if k == 1:
                in_a[...] = answer[0, 1, SUB]

        @pl.when(base == 0)
        def _():
            early(1)
            for q in range(SUB + 1, 0, -1):
                if q != SUB:
                    a_copy(1, q).start()
            in_a[...] = answer[0, 1, SUB]
            pl.semaphore_wait(ready, 1)
            hop_copy(1).start()
            early(0)
            tell(0)

        @pl.when(base != 0)
        def _():
            pl.semaphore_wait(ready, 1)
            early(0)
            early(1)
            tell(0)
            tell(1)

    def arrived_right(k):
        arrived_map(k, LEFT - 1, 0)
        arrived_vec(k, LEFT - 1, 0)
        for q in range(LEFT, CUT):
            def arrived(q=q):
                for m in range(3):
                    arrived_map(k, q, m)
                for m in range(2):
                    arrived_vec(k, q, m)

            unless_mid(k, q, arrived)
        for q in range(CUT - 2, LEFT - 1, -1):
            c_maps[k, q - LEFT, 1] = mm(c_maps[k, q, 1], c_maps[k, q + 1, 1] if q == CUT - 2 else c_maps[k, q + 1 - LEFT, 1])

        @pl.when(base == 0)
        def _():
            arrived_map(k, 0, 2)

        @pl.when(base != 0)
        def _():
            c_maps[k, 0, 2] = jnp.zeros((NC, NC, 4, 128), jnp.float32)
            c_vecs[k, 0, 1] = jnp.zeros((NC, 4, 128), jnp.float32)

    def right_values(k, a, stop):
        for q in range(LEFT, CUT):
            answer[0, k, q] = a
            a = mv(c_maps[k, q, 0], a) + c_vecs[k, q, 0]
        answer[0, k, CUT] = a
        b = mv(c_maps[k, 0, 2], a)
        answer[1, k, CUT - 1] = b
        for q in range(CUT - 1, stop, -1):
            b = mv(c_maps[k, q, 1], b) + mv(c_maps[k, q, 2], answer[0, k, q]) + c_vecs[k, q, 1]
            answer[1, k, q - 1] = b

    def heard(k):
        hop_copy(k).wait_recv()
        answer[0, k, LEFT - 1] = hop_in[k]
        return mv(c_maps[k, LEFT - 1, 0], hop_in[k]) + c_vecs[k, LEFT - 1, 0]

    def solve(k):
        arrived_right(k)
        a = heard(k)
        right_values(k, a, LEFT - 1)

    def prepare(k):
        arrived_right(k)
        back = c_maps[k, 0, 2]
        for q in range(CUT - 1, LEFT - 1, -1):
            back = c_maps[k, q, 2] + mm(c_maps[k, q, 1], mm(back, c_maps[k, q, 0]))
        c_maps[k, LEFT - 2, 1] = mm(back, c_maps[k, LEFT - 1, 0])
        right_values(k, c_vecs[k, LEFT - 1, 0], LEFT - 1)

    def finish(k, late):
        if late:
            hop_copy(k).wait_recv()
            answer[1, k, LEFT - 1] = answer[1, k, LEFT - 1] + mv(c_maps[k, LEFT - 2, 1], hop_in[k])

        @pl.when(base == 0)
        def _():
            arrived_vec(k, 0, 1)

        w = c_vecs[k, 0, 1]
        answer[1, k, LEFT - 1] = answer[1, k, LEFT - 1] + mv(c_maps[k, 0, 1], w)
        b_copy(k, 0).start()

    def finish_left(cores):
        for j in range(1, LEFT):
            for k in cores:
                b_copy(k, j).start()

    def finish_right(k, late):
        if late:
            right_values(k, mv(c_maps[k, LEFT - 1, 0], hop_in[k]) + c_vecs[k, LEFT - 1, 0], LEFT)
        w = c_vecs[k, 0, 1]
        for q in range(LEFT, CUT):
            if q == CUT - 1:
                more = w
            else:
                more = mv(c_maps[k, CUT - 1, 1] if q == CUT - 2 else c_maps[k, q + 1 - LEFT, 1], w)
            answer[1, k, q] = answer[1, k, q] + more

            def answers(q=q):
                b_copy(k, q).start()
                a_copy(k, q).start()

            unless_mid(k, q, answers)

        @pl.when(base == 0)
        def _():
            a_copy(k, CUT).start()

        if k == 1:
            in_a[...] = answer[0, 1, mid]
            in_b[...] = answer[1, 1, mid]

    @pl.when(is_mid)
    def _():
        c_maps[1, mid] = maps[...]
        c_vecs[1, mid] = vecs[...]

        @pl.when(base != 0)
        def _():
            prepare(1)
            prepare(0)
            finish(0, True)
            finish(1, True)
            finish_left((0, 1))
            finish_right(0, True)
            finish_right(1, True)

        @pl.when((base == 0) & (pair == 0))
        def _():
            solve(1)
            finish(1, False)
            prepare(0)
            finish(0, True)
            finish_left((0, 1))
            finish_right(1, False)
            finish_right(0, True)

        @pl.when((base == 0) & (pair != 0))
        def _():
            solve(1)
            solve(0)
            finish(0, False)
            finish(1, False)
            finish_left((0, 1))
            finish_right(0, False)
            finish_right(1, False)

    @pl.when(jnp.logical_not(is_mid | is_sub) & (st != 0))
    def _():
        a_copy(0, 1).wait_recv()

    @pl.when(st == 0)
    def _():
        in_a[...] = jnp.zeros((NC, 4, 128), jnp.float32)

    a_in = in_a[...]

    def side_y_copy(q):
        return pltpu.make_async_remote_copy(
            y_out, side_y.at[pos], sys_sem.at[q], syr_sem.at[pos], **to(base + q, pt)
        )

    @pl.when(left & (pos > 0))
    def _():
        @pl.when(unheard)
        def _():
            side_b_copy(0).start()

        y_out[...] = mv(maps[2], a_in) + vecs[1]
        for q in range(LEFT - 1):
            @pl.when(pos > q)
            def _():
                side_y_copy(q).start()

    a1 = jnp.where(is_cut, ghost[...], mv(m0, a_in) + v0)
    vh[0, :, 0:4, :] = a_in
    vh[0, :, 4:8, :] = a1
    a_h = vh[0]
    for i in range(8):
        part = flow_v[:, pl.ds(i, 8, stride=8), :] + c_v[i] + mv(p_v[i], a_h)
        for c in range(NC):
            outs[c][pl.ds(i, 8, stride=8), :] = part[c]
    half_b = mv(w1, a1) + ww1

    for e in range(1, LEFT):
        @pl.when(pos < e)
        def _():
            pltpu.make_async_copy(maps.at[1], side_b.at[e], sbr_sem.at[e]).wait()
            pltpu.make_async_copy(y_out, side_y.at[e], syr_sem.at[e]).wait()

    for e in range(LEFT - 1, 1, -1):
        @pl.when(pos < e - 1)
        def _():
            side_y[e - 1] = mv(side_b[e - 1], side_y[e]) + side_y[e - 1]
            side_b[e - 1] = mm(side_b[e - 1], side_b[e])

    @pl.when(jnp.logical_not(is_mid))
    def _():
        b_copy(0, 0).wait_recv()

    for e in range(1, LEFT):
        @pl.when(pos == e - 1)
        def _():
            in_b[...] = mv(side_b[e], in_b[...]) + side_y[e]

    b_in = in_b[...] * jnp.where(st == NS - 1, 0.0, 1.0)
    vh[1, :, 0:4, :] = (mv(b1, b_in) + half_b) * keep
    vh[1, :, 4:8, :] = b_in
    b_h = vh[1]

    def out_copy(c):
        return pltpu.make_async_copy(outs[c], out.at[c], out_sem.at[c])

    for c in range(NC):
        for i in range(8):
            outs[c][pl.ds(i, 8, stride=8), :] = outs[c][pl.ds(i, 8, stride=8), :] + sum(
                q_v[i, c, k] * b_h[k] for k in range(NC)
            )
        out_copy(c).start()

    for c in range(NC):
        out_copy(c).wait()

    @pl.when(((pos > 0) & left & jnp.logical_not(is_sub)) | near)
    def _():
        map_copy(0).wait_send()

    @pl.when(is_sub)
    def _():
        for k in range(2):
            hop_copy(k).wait_send()
            for q in range(1, SUB + 2):
                if (k, q) != (1, SUB):
                    a_copy(k, q).wait_send()

    @pl.when(near)
    def _():
        map_copy(1).wait_send()

    @pl.when(near | is_cut)
    def _():
        map_copy(2).wait_send()
        w_copy(centre, pos).wait_send()

    @pl.when(jnp.logical_not(is_mid | is_sub))
    def _():
        v_copy().wait_send()

    for q in range(LEFT - 1):
        @pl.when(left & (pos > q))
        def _():
            side_b_copy(q).wait_send()
            side_y_copy(q).wait_send()

    @pl.when(is_mid)
    def _():
        for k, q in a_sent:
            if LEFT <= q < CUT:
                unless_mid(k, q, lambda k=k, q=q: a_copy(k, q).wait_send())


        @pl.when(base == 0)
        def _():
            for k in range(2):
                a_copy(k, CUT).wait_send()

        for k, q in b_sent:
            unless_mid(k, q, lambda k=k, q=q: b_copy(k, q).wait_send())


def to_tiles(x):
    lead = x.shape[:-2]
    x = x.reshape(lead + (2, 8, 4, 128))
    n = len(lead)
    x = jnp.transpose(x, tuple(range(n)) + (n, n + 2, n + 1, n + 3))
    return x.reshape(lead + (64, 128))


def from_tiles(x):
    lead = x.shape[:-2]
    x = x.reshape(lead + (2, 4, 8, 128))
    n = len(lead)
    x = jnp.transpose(x, tuple(range(n)) + (n, n + 2, n + 1, n + 3))
    return x.reshape(lead + (16, 512))


def local(flow_state, residual, spread, diag_inv, lower_jac, upper_jac, partner):
    f32 = jnp.float32
    vm = lambda *s: pltpu.VMEM(s, f32)
    dma = lambda *n: pltpu.SemaphoreType.DMA(n)
    hbm = pl.BlockSpec(memory_space=pltpu.HBM)
    updated = pl.pallas_call(
        kernel,
        out_shape=jax.ShapeDtypeStruct((NC, 64, 128), f32),
        in_specs=[hbm] * 7,
        out_specs=hbm,
        scratch_shapes=[
            vm(64, 128), vm(64, 128), vm(64, 128), vm(64, 128), vm(64, 128), dma(NC),
            vm(5, 64, 128), vm(5, 64, 128), vm(64, 128), vm(25, 64, 128), vm(25, 64, 128), vm(25, 64, 128), vm(5, 64, 128),
            vm(8, 5, 5, 8, 128), vm(8, 5, 5, 8, 128), vm(8, 5, 5, 8, 128), vm(8, 5, 5, 8, 128), vm(8, 5, 5, 8, 128), vm(8, 5, 8, 128),
            vm(5, 2, 8, 128), vm(5, 2, 8, 128), vm(ROW, 5, 4, 128), vm(5, 4, 128), vm(3, 5, 4, 128), vm(4, 5, 4, 128), vm(5, 4, 128),
            vm(3, 5, 5, 4, 128), vm(2, 5, 4, 128), vm(2, 5, 8, 128),
            vm(2, CUT, 3, 5, 5, 4, 128), vm(2, CUT, 2, 5, 4, 128), vm(2, 2, CUT + 1, 5, 4, 128),
            vm(5, 4, 128), vm(5, 4, 128), vm(LEFT, 5, 5, 4, 128), vm(LEFT, 5, 4, 128), vm(5, 4, 128), vm(2, 5, 4, 128),
            pltpu.SMEM((128,), jnp.int32), dma(7), dma(4), dma(4), dma(ROW), dma(ROW), dma(3), dma(3), pltpu.SemaphoreType.REGULAR, pltpu.SemaphoreType.REGULAR,
            dma(3), dma(2, CUT, 3), dma(2), dma(2, CUT, 2), dma(LEFT), dma(LEFT), dma(LEFT), dma(LEFT),
            dma(2, CUT + 1), dma(1), dma(2, CUT + 1), dma(1), dma(2), dma(2),
        ],
        compiler_params=pltpu.CompilerParams(
            collective_id=0, has_side_effects=True, vmem_limit_bytes=60 * 1024 * 1024
        ),
        name="lusgs",
    )(
        to_tiles(flow_state), to_tiles(residual), to_tiles(spread), to_tiles(diag_inv),
        to_tiles(lower_jac), to_tiles(upper_jac), partner,
    )
    return from_tiles(updated)


def solution(mesh):
    blocks = P(None, "stream", "pitch")
    in_specs = (blocks, blocks, P("stream", "pitch"), blocks, blocks, blocks, P())
    return jax.shard_map(local, mesh=mesh, in_specs=in_specs, out_specs=blocks, check_vma=False)
```
